128 devices in a mesh: dp: 2 (over z_lo), fsdp: 64 (over y, z_hi, x, core).
Axes of the slice: x: 4, y: 4, z: 4 (z_hi: 2, z_lo: 2; z = z_hi * 2 + z_lo), core: 2. Of those that a mesh axis runs over, the one named last changes fastest.
Arguments:
- tokens: bfloat16 [256, 64, 2048], P(('dp', 'fsdp')), may hold values from -6 to 6
- segments: int32 [256, 64], P(('dp', 'fsdp')), may hold values from 0 to 7, never falling along the last dimension, each value on 1 to 32 neighbouring positions
- qkv_weight: bfloat16 [2048, 4096], P('fsdp'), may hold values from -0.125 to 0.125
- out_weight: bfloat16 [2048, 2048], P('fsdp'), may hold values from -0.25 to 0.25
- attn_gain: bfloat16 [2048], P('fsdp'), may hold values from 0.25 to 1.75
- query_gain: bfloat16 [128], P('fsdp'), may hold values from 0.25 to 1.75
- key_gain: bfloat16 [128], P('fsdp'), may hold values from 0.25 to 1.75
- ffn_weight: bfloat16 [2048, 12288], P('fsdp'), may hold values from -0.125 to 0.125
- down_weight: bfloat16 [6144, 2048], P('fsdp'), may hold values from -0.078125 to 0.078125
- ffn_gain: bfloat16 [2048], P('fsdp'), may hold values from 0.25 to 1.75
- out_grad: bfloat16 [256, 64, 2048], P(('dp', 'fsdp')), may hold values from -6 to 6
Outputs:
- result: bfloat16 [256, 64, 2048], P(('dp', 'fsdp'))
- tokens_grad: float32 [256, 64, 2048], P(('dp', 'fsdp'))
- qkv_weight_grad: float32 [2048, 4096], P('fsdp')
- out_weight_grad: float32 [2048, 2048], P('fsdp')
- attn_gain_grad: float32 [2048], P('fsdp')
- query_gain_grad: float32 [128], P('fsdp')
- key_gain_grad: float32 [128], P('fsdp')
- ffn_weight_grad: float32 [2048, 12288], P('fsdp')
- down_weight_grad: float32 [6144, 2048], P('fsdp')
- ffn_gain_grad: float32 [2048], P('fsdp')
The draws below stay inside these ranges and needn't reach their ends.
Inputs may be any that keep to these rules, and one draw needn't show every extreme that they name: `segments`: within each sequence the segment numbers never fall; every document holds 1 to 32 tokens, and one holds exactly 32.
All inputs are finite; a program needn't handle non-finite values.
Results may differ from the reference program's by a relative error of at most 0.024.
Values may be sent and summed in bfloat16 or wider, within the bound.
No kernel may reach another device: no remote copies, remote signals or barrier semaphores. Data moves between devices by JAX's collectives and lax.ppermute only.
A program may use at most 512 MiB of HBM per device.

```python
import math
import jax
import jax.numpy as jnp
import numpy as np
from jax import lax

D = 2048
H = 16
KVH = 8
HD = 128
FF = 6144
SEQ = 64
QKV = 4096
SEQS = 256


def steps_of(key, dims, cuts, least, high):
    def one(position, parts):
        steps = jax.random.uniform(jax.random.fold_in(jax.random.fold_in(key, 6), position), (parts,), jnp.float32, least / len(cuts), high / len(cuts))
        return jnp.repeat(jnp.exp(steps), dims[position] // parts).reshape((-1,) + (1,) * (len(dims) - position - 1))

    level = one(*cuts[0])
    for cut in cuts[1:]:
        level = level * one(*cut)
    return level


def length_profile(amount, total, limit, lean):
    portions = [(1 << 20) // math.isqrt(standing ** lean) + 1 for standing in range(2, amount + 1)]
    spare, counts = total - limit - (amount - 1), [1] * (amount - 1)
    while spare > 0:
        free = [i for i in range(amount - 1) if counts[i] < limit]
        mass, budget = sum([portions[i] for i in free]), spare
        for i in free:
            addition = min(limit - counts[i], max(1, budget * portions[i] // mass), spare)
            counts[i] = counts[i] + addition
            spare = spare - addition
    return np.array([limit] + counts)


def uneven_parts(key, number_of, total, bound, skew):
    if number_of == 2:
        one = jax.random.randint(key, (), max(1, total - bound), min(bound, total - 1) + 1)
        return jnp.stack([one, total - one])
    lengths = jnp.asarray(length_profile(number_of, total, bound, skew), jnp.int32)
    couples = (number_of - 1) // 2
    giver, receiver = lengths[1:1 + 2 * couples:2], lengths[2:2 + 2 * couples:2]
    margin = jnp.minimum(giver - 1, bound - receiver)
    passed = jax.random.randint(jax.random.fold_in(key, 1), (couples,), 0, 1 << 20) % (margin + 1)
    lengths = lengths.at[1:1 + 2 * couples:2].set(giver - passed).at[2:2 + 2 * couples:2].set(receiver + passed)
    return lengths[jax.random.permutation(jax.random.fold_in(key, 2), number_of)]


def normal_values(stream_key, shape, width, most, cuts=(), kind=jnp.bfloat16):
    level = steps_of(stream_key, shape, cuts, -0.22, 0.18) if cuts else 1.0
    array = jax.random.normal(stream_key, shape, jnp.float32) * width * level
    return jnp.minimum(jnp.maximum(array, -most), most).astype(kind)


def setup_inputs(seed: int = 0) -> dict:
    streams_of = jax.random.split(jax.random.key(seed), 12)
    tokens = normal_values(streams_of[0], (SEQS, SEQ, D), 1.0, 6.0, ((0, 128),))
    segments = jax.vmap(lambda own: jnp.searchsorted(jnp.cumsum(uneven_parts(own, max(3, SEQ // 8), SEQ, SEQ // 2, 1)), jnp.arange(SEQ), side="right"))(jax.random.split(streams_of[1], SEQS)).reshape((SEQS, SEQ)).astype(jnp.int32)
    qkv_weight = normal_values(streams_of[2], (D, QKV), D ** -0.5, 0.125, ((0, 64),))
    out_weight = normal_values(streams_of[3], (H * HD, D), (H * HD // 4) ** -0.5, 0.25, ((0, 64),))
    attn_gain = jnp.clip(1.0 + 0.15 * jax.random.normal(streams_of[4], (D,), jnp.float32), 0.25, 1.75).astype(jnp.bfloat16)
    query_gain = jnp.clip(1.0 + 0.15 * jax.random.normal(streams_of[5], (HD,), jnp.float32), 0.25, 1.75).astype(jnp.bfloat16)
    key_gain = jnp.clip(1.0 + 0.15 * jax.random.normal(streams_of[6], (HD,), jnp.float32), 0.25, 1.75).astype(jnp.bfloat16)
    ffn_weight = normal_values(streams_of[7], (D, 2 * FF), D ** -0.5, 0.125, ((0, 64),))
    down_weight = normal_values(streams_of[8], (FF, D), FF ** -0.5, 0.078125, ((0, 64),))
    ffn_gain = jnp.clip(1.0 + 0.15 * jax.random.normal(streams_of[9], (D,), jnp.float32), 0.25, 1.75).astype(jnp.bfloat16)
    out_grad = normal_values(streams_of[10], (SEQS, SEQ, D), 1.0, 6.0, ((0, 128),))
    return {"tokens": tokens, "segments": segments, "qkv_weight": qkv_weight, "out_weight": out_weight, "attn_gain": attn_gain, "query_gain": query_gain, "key_gain": key_gain, "ffn_weight": ffn_weight, "down_weight": down_weight, "ffn_gain": ffn_gain, "out_grad": out_grad}


@jax.custom_vjp
def low(v):
    return lax.optimization_barrier(v.astype(jnp.bfloat16)).astype(jnp.float32)

@jax.custom_vjp
def low_back(v):
    return v

def low_keep(v):
    return (low(v), None)

def low_pass(kept, grad):
    return (grad,)

def back_keep(v):
    return (v, None)

def back_low(kept, grad):
    return (low(grad),)
low.defvjp(low_keep, low_pass)
low_back.defvjp(back_keep, back_low)
epsilon = 1e-06
neg_large = -1e+30
rope_base = 1000000.0
highest = lax.Precision.HIGHEST

def normed(values, gain_vec):
    return values * lax.rsqrt(lax.optimization_barrier(jnp.mean(values * values, axis=-1, keepdims=True)) + epsilon) * gain_vec

def doc_positions(segments):
    length = segments.shape[-1]
    places = jnp.broadcast_to(jnp.arange(length, dtype=jnp.int32), segments.shape)
    starts = jnp.concatenate([jnp.ones(segments.shape[:-1] + (1,), jnp.bool_), segments[..., 1:] != segments[..., :-1]], axis=-1)
    first_place = lax.cummax(jnp.where(starts, places, 0), axis=segments.ndim - 1)
    return places - first_place

def rope_tables(positions, head_dim):
    half_dim = head_dim // 2
    frequency = rope_base ** (-(jnp.arange(half_dim, dtype=jnp.float32) * 2.0 / head_dim))
    angles = positions.astype(jnp.float32)[..., None] * frequency
    angles = jnp.concatenate([angles, angles], axis=-1)
    return (jnp.cos(angles), jnp.sin(angles))

def rotate(values, cosine, sine_table):
    half_dim = values.shape[-1] // 2
    turned = jnp.concatenate([-values[..., half_dim:], values[..., :half_dim]], axis=-1)
    return values * cosine + turned * sine_table

def layer_block(inputs, segments, params):
    qkv_weight, out_weight, attn_gain, query_gain, key_gain, ffn_weight, down_weight, ffn_gain = params
    seq_count = inputs.shape[0]
    length = inputs.shape[1]
    normal_in = low(normed(inputs, attn_gain))
    qkv_proj = low_back(jnp.einsum('nsd,de->nse', normal_in, qkv_weight, precision=highest))
    queries = qkv_proj[..., :H * HD].reshape(seq_count, length, H, HD)
    key_part = qkv_proj[..., H * HD:(H + KVH) * HD].reshape(seq_count, length, KVH, HD)
    value_part = qkv_proj[..., (H + KVH) * HD:].reshape(seq_count, length, KVH, HD)
    cosine, sine_table = rope_tables(doc_positions(segments), HD)
    cosine = cosine[:, :, None, :]
    sine_table = sine_table[:, :, None, :]
    query_rot = low(rotate(normed(queries, query_gain), cosine, sine_table)).reshape(seq_count, length, KVH, H // KVH, HD)
    key_rot = low(rotate(normed(key_part, key_gain), cosine, sine_table))
    value_low = low(value_part)
    scores = jnp.einsum('nahgd,nbhd->nhgab', query_rot, key_rot, precision=highest) * HD ** (-0.5)
    places = jnp.arange(length)
    allowed = (segments[:, :, None] == segments[:, None, :]) & (places[None, None, :] <= places[None, :, None])
    scores = low_back(jnp.where(allowed[:, None, None], scores, neg_large))
    shifted = scores - lax.optimization_barrier(jnp.max(scores, axis=-1, keepdims=True))
    exp_scores = jnp.exp(shifted)
    probabilities = low(exp_scores / lax.optimization_barrier(jnp.sum(exp_scores, axis=-1, keepdims=True)))
    mixed_heads = jnp.einsum('nhgab,nbhd->nahgd', probabilities, value_low, precision=highest).reshape(seq_count, length, H * HD)
    mixed_heads = low(low_back(mixed_heads))
    hidden = inputs + low_back(jnp.einsum('nse,ed->nsd', mixed_heads, out_weight, precision=highest))
    normal_mid = low(normed(hidden, ffn_gain))
    gate_up = low_back(jnp.einsum('nsd,df->nsf', normal_mid, ffn_weight, precision=highest))
    gate_part = gate_up[..., :FF]
    upward = gate_up[..., FF:]
    active = low(gate_part * jax.nn.sigmoid(gate_part) * upward)
    return hidden + low_back(jnp.einsum('nsf,fd->nsd', active, down_weight, precision=highest))

def reference(tokens, segments, qkv_weight, out_weight, attn_gain, query_gain, key_gain, ffn_weight, down_weight, ffn_gain, out_grad):
    group_size = math.gcd(SEQS, max(1, 4096 // SEQ))
    blocks = SEQS // group_size
    seg_blocks = segments.reshape(blocks, group_size, SEQ)

    def forward(inputs, *params):
        pieces = inputs.reshape(blocks, group_size, SEQ, D)
        block_fn = jax.checkpoint(lambda pair_in: layer_block(pair_in[0], pair_in[1], params))
        return lax.map(block_fn, (pieces, seg_blocks)).reshape(SEQS, SEQ, D)
    floats = [tokens.astype(jnp.float32), qkv_weight.astype(jnp.float32), out_weight.astype(jnp.float32), attn_gain.astype(jnp.float32), query_gain.astype(jnp.float32), key_gain.astype(jnp.float32), ffn_weight.astype(jnp.float32), down_weight.astype(jnp.float32), ffn_gain.astype(jnp.float32)]
    result, pullback = jax.vjp(forward, *floats)
    gradients = pullback(out_grad.astype(jnp.float32))
    return (result.astype(jnp.bfloat16), gradients[0], gradients[1], gradients[2], gradients[3], gradients[4], gradients[5], gradients[6], gradients[7], gradients[8])
```

```python
import itertools

import jax
import jax.numpy as jnp
import numpy as np
from jax import lax
from jax.experimental import pallas as pl
from jax.experimental.pallas import tpu as pltpu
from jax.sharding import Mesh
from jax.sharding import PartitionSpec as P

D = 2048
H = 16
KVH = 8
HD = 128
FF = 6144
SEQ = 64
RANKS = 8
QCOLS = 2 * HD
CCOLS = 4 * HD
FCOLS = FF // RANKS
BLOCK = 256
SUB = 128

EPS = 1e-06
NEG = -1e30
BASE = 1000000.0
SCALE = HD**-0.5
BF = jnp.bfloat16
F32 = jnp.float32

AXES = ("zl", "y", "zh", "x", "c")
SIZES = {"zl": 2, "y": 4, "zh": 2, "x": 4, "c": 2}


def place(d):
    i = 0
    for a in AXES:
        i = i * SIZES[a] + d[a]
    return i


def pairs(move):
    found = []
    for t in itertools.product(*[range(SIZES[a]) for a in AXES]):
        d = dict(zip(AXES, t))
        e = move(dict(d))
        if e is not None:
            found.append((place(d), place(e)))
    return found


def step(axis, by):
    def move(d):
        if axis == "z":
            z = (d["zh"] * 2 + d["zl"] + by) % 4
            d["zh"], d["zl"] = z // 2, z % 2
        else:
            d[axis] = (d[axis] + by) % SIZES[axis]
        return d

    return move


def send(v, move):
    return lax.ppermute(v, AXES, pairs(move))


def partner(d):
    d["zl"], d["zh"] = 1 - d["zl"], 1 - d["zh"]
    return d


def spread_rows(half):
    def move(d):
        if d["y"] // 2 != d["zl"]:
            return None
        return {
            "zl": d["zl"],
            "y": d["x"],
            "zh": d["zh"],
            "x": 2 * d["c"] + half,
            "c": d["y"] % 2,
        }

    return move


def collect_rows(half):
    def move(d):
        if d["x"] % 2 != half:
            return None
        return {
            "zl": d["zl"],
            "y": 2 * d["zl"] + d["c"],
            "zh": d["zh"],
            "x": d["y"],
            "c": d["x"] // 2,
        }

    return move


def share_rows(d):
    if d["y"] // 2 != d["zl"]:
        return None
    d["zl"] = 1 - d["zl"]
    return d


def ring(v, axis):
    return [
        v,
        send(v, step(axis, -1)),
        send(v, step(axis, 2)),
        send(v, step(axis, 1)),
    ]


def gather_group(v):
    same = jnp.concatenate(ring(v, "z"), axis=0)
    return jnp.concatenate([same, send(same, step("c", 1))], axis=0)


def sum_group(parts, rows):
    half = 4 * rows
    other = send(parts[half:], step("c", 1))
    both = parts[:half].astype(F32) + other.astype(F32)
    low = both.astype(BF)
    one = send(low[rows : 2 * rows], step("z", 1))
    two = send(low[2 * rows : 3 * rows], step("z", 2))
    three = send(low[3 * rows :], step("z", -1))
    return (
        both[:rows] + one.astype(F32) + two.astype(F32) + three.astype(F32)
    )


def in_order(found, mine):
    twice = jnp.stack(found + found, axis=0)
    return lax.dynamic_slice_in_dim(twice, 4 - mine, 4, axis=0)


def last(a, b):
    return lax.dot_general(a, b, (((1,), (1,)), ((), ())), preferred_element_type=F32)


def first(a, b):
    return lax.dot_general(a, b, (((0,), (0,)), ((), ())), preferred_element_type=F32)


def plain(a, b):
    return jnp.dot(a, b, preferred_element_type=F32)


def root(v):
    return lax.rsqrt(jnp.mean(v * v, axis=-1, keepdims=True) + EPS)


def rotate(v, cos, sin):
    return v * cos + pltpu.roll(v, HD // 2, 1) * sin


def unrotate(v, cos, sin):
    return v * cos + pltpu.roll(v * sin, HD // 2, 1)


def scores_of(query, key, keep):
    s = last(query, key) * SCALE
    s = jnp.where(keep, s, NEG)
    p = jnp.exp(s - jnp.max(s, axis=-1, keepdims=True))
    return p / jnp.sum(p, axis=-1, keepdims=True)


def keep_mask(doc_col, doc_row):
    shape = (SUB, SUB)
    a = lax.broadcasted_iota(jnp.int32, shape, 0)
    b = lax.broadcasted_iota(jnp.int32, shape, 1)
    keep = (doc_col == doc_row) & (b <= a)
    return jnp.concatenate([keep, keep], axis=0)


def heads_of(qkv, gains, cos, sin):
    q0, q1, k = qkv[:, :HD], qkv[:, HD:QCOLS], qkv[:, QCOLS : QCOLS + HD]
    gq, gk = gains[0:1], gains[1:2]
    r0, r1, rk = root(q0), root(q1), root(k)
    z0, z1, zk = q0 * r0, q1 * r1, k * rk
    a0 = rotate(z0 * gq, cos, sin).astype(BF)
    a1 = rotate(z1 * gq, cos, sin).astype(BF)
    ak = rotate(zk * gk, cos, sin).astype(BF)
    val = qkv[:, QCOLS + HD :].astype(BF)
    return (r0, r1, rk), (z0, z1, zk), (a0, a1, ak), val


def attn_forward(x, w, wo, dcol, drow, cos, sin, gains, z_out, qkv_out, mix_out, part_out):
    xf = x[...].astype(F32)
    z = (xf * root(xf)).astype(BF)
    z_out[...] = z
    qkv = plain(z, w[...])
    qkv_out[...] = qkv
    _, _, (a0, a1, ak), val = heads_of(qkv, gains[...], cos[...], sin[...])
    for s in range(BLOCK // SUB):
        r = slice(s * SUB, (s + 1) * SUB)
        keep = keep_mask(dcol[r, :], drow[0, :, r])
        p = scores_of(jnp.concatenate([a0[r], a1[r]], axis=0), ak[r], keep)
        o = plain(p.astype(BF), val[r])
        mix_out[r, :HD] = o[:SUB].astype(BF)
        mix_out[r, HD:] = o[SUB:].astype(BF)
    part_out[...] = plain(mix_out[...], wo[...]).astype(BF)


def norm_back(r, z, gain, e):
    eg = e * gain
    return r * (eg - z * jnp.mean(eg * z, axis=-1, keepdims=True)), jnp.sum(
        e * z, axis=0, keepdims=True
    )


def attn_backward(g, qkv_in, w, wo, dcol, drow, cos, sin, gains, gqkv_out, part_out, gain_out):
    gm = last(g[...], wo[...]).astype(BF)
    gain = gains[...]
    c, s_ = cos[...], sin[...]
    (r0, r1, rk), (z0, z1, zk), (a0, a1, ak), val = heads_of(qkv_in[...], gain, c, s_)
    d0, d1, dk, dv = [], [], [], []
    for s in range(BLOCK // SUB):
        r = slice(s * SUB, (s + 1) * SUB)
        keep = keep_mask(dcol[r, :], drow[0, :, r])
        q = jnp.concatenate([a0[r], a1[r]], axis=0)
        do = jnp.concatenate([gm[r, :HD], gm[r, HD:]], axis=0)
        p = scores_of(q, ak[r], keep)
        dp = last(do, val[r])
        ds = (p * (dp - jnp.sum(p * dp, axis=-1, keepdims=True))).astype(BF)
        dq = plain(ds, ak[r]) * SCALE
        d0.append(dq[:SUB])
        d1.append(dq[SUB:])
        dk.append(first(ds, q) * SCALE)
        dv.append(first(p.astype(BF), do))
    d0, d1, dk, dv = [jnp.concatenate(v, axis=0) for v in (d0, d1, dk, dv)]
    g0, t0 = norm_back(r0, z0, gain[0:1], unrotate(d0, c, s_))
    g1, t1 = norm_back(r1, z1, gain[0:1], unrotate(d1, c, s_))
    gk, tk = norm_back(rk, zk, gain[1:2], unrotate(dk, c, s_))
    gqkv_out[:, :HD] = g0.astype(BF)
    gqkv_out[:, HD:QCOLS] = g1.astype(BF)
    gqkv_out[:, QCOLS : QCOLS + HD] = gk.astype(BF)
    gqkv_out[:, QCOLS + HD :] = dv.astype(BF)
    part_out[...] = last(gqkv_out[...], w[...]).astype(BF)

    @pl.when(pl.program_id(0) == 0)
    def _():
        gain_out[...] = jnp.zeros_like(gain_out)

    gain_out[0:1] += t0 + t1
    gain_out[1:2] += tk


def whole(*shape):
    return pl.BlockSpec(shape, lambda i: (0,) * len(shape))


def rows_of(width):
    return pl.BlockSpec((BLOCK, width), lambda i: (i, 0))


PARAMS = pltpu.CompilerParams(
    dimension_semantics=("arbitrary",), vmem_limit_bytes=48 * 1024 * 1024
)


def call_forward(x, w, wo, dcol, drow, cos, sin, gains):
    n = x.shape[0]
    return pl.pallas_call(
        attn_forward,
        grid=(n // BLOCK,),
        in_specs=[
            rows_of(D),
            whole(D, CCOLS),
            whole(QCOLS, D),
            rows_of(1),
            pl.BlockSpec((1, 1, BLOCK), lambda i: (i, 0, 0)),
            whole(BLOCK, HD),
            whole(BLOCK, HD),
            whole(8, HD),
        ],
        out_specs=[rows_of(D), rows_of(CCOLS), rows_of(QCOLS), rows_of(D)],
        out_shape=[
            jax.ShapeDtypeStruct((n, D), BF),
            jax.ShapeDtypeStruct((n, CCOLS), F32),
            jax.ShapeDtypeStruct((n, QCOLS), BF),
            jax.ShapeDtypeStruct((n, D), BF),
        ],
        compiler_params=PARAMS,
        cost_estimate=pl.CostEstimate(
            flops=2 * n * D * (CCOLS + QCOLS), bytes_accessed=16 << 20, transcendentals=n * 256
        ),
    )(x, w, wo, dcol, drow, cos, sin, gains)


def call_backward(g, qkv, w, wo, dcol, drow, cos, sin, gains):
    n = g.shape[0]
    return pl.pallas_call(
        attn_backward,
        grid=(n // BLOCK,),
        in_specs=[
            rows_of(D),
            rows_of(CCOLS),
            whole(D, CCOLS),
            whole(QCOLS, D),
            rows_of(1),
            pl.BlockSpec((1, 1, BLOCK), lambda i: (i, 0, 0)),
            whole(BLOCK, HD),
            whole(BLOCK, HD),
            whole(8, HD),
        ],
        out_specs=[rows_of(CCOLS), rows_of(D), whole(8, HD)],
        out_shape=[
            jax.ShapeDtypeStruct((n, CCOLS), BF),
            jax.ShapeDtypeStruct((n, D), BF),
            jax.ShapeDtypeStruct((8, HD), F32),
        ],
        compiler_params=PARAMS,
        cost_estimate=pl.CostEstimate(
            flops=2 * n * D * (CCOLS + QCOLS), bytes_accessed=16 << 20, transcendentals=n * 256
        ),
    )(g, qkv, w, wo, dcol, drow, cos, sin, gains)


def tables():
    half = HD // 2
    freq = BASE ** (-(np.arange(half, dtype=np.float64) * 2.0 / HD))
    angles = np.arange(SEQ, dtype=np.float64)[:, None] * freq
    cos = np.concatenate([np.cos(angles)] * 2, axis=-1)
    sin = np.concatenate([-np.sin(angles), np.sin(angles)], axis=-1)
    reps = (BLOCK // SEQ, 1)
    return np.tile(cos, reps).astype(np.float32), np.tile(sin, reps).astype(np.float32)


def rank_pieces(shard, cuts):
    made = []
    for zl, zh, c in itertools.product(range(2), range(2), range(2)):
        t = 4 * zl + 2 * c + zh
        made.append(
            jnp.concatenate(
                [shard[:, at + t * width : at + (t + 1) * width] for at, width in cuts],
                axis=1,
            )
        )
    return jnp.stack(made).reshape((2, 2, 2) + made[0].shape)


def pick(v, *at):
    for i in at:
        v = lax.dynamic_index_in_dim(v, i, 0, keepdims=False)
    return v


def my_columns(shard, cuts, zl, zh, c):
    pieces = rank_pieces(shard, cuts)
    near, far = pick(pieces, zl, zh), pick(pieces, 1 - zl, 1 - zh)
    keep = jnp.stack([pick(near, c), pick(far, c)])
    give = jnp.stack([pick(near, 1 - c), pick(far, 1 - c)])
    got = send(give, step("c", 1))
    by_c = jnp.where(
        c == 0, jnp.stack([keep, got], axis=1), jnp.stack([got, keep], axis=1)
    )
    beyond = send(by_c[1], partner)
    mine = by_c[0]
    return jnp.where(
        zh == 0, jnp.stack([mine, beyond]), jnp.stack([beyond, mine])
    )


def own_rows(part, cuts, columns, zl, zh, c):
    z = 2 * zh + zl

    def to(by):
        return pick(part, ((z + by) % 4) // 2)

    found = [
        to(0),
        send(to(-1), step("z", -1)),
        send(to(2), step("z", 2)),
        send(to(1), step("z", 1)),
    ]
    by_z = in_order(found, z)
    by_z = by_z.reshape((2, 2) + by_z.shape[1:])
    keep = lax.dynamic_index_in_dim(by_z, c, 2, keepdims=False)
    give = lax.dynamic_index_in_dim(by_z, 1 - c, 2, keepdims=False)
    got = send(give, step("c", 1))
    low = jnp.where(c == 0, keep, got)
    high = jnp.where(c == 0, got, keep)
    made = []
    at = 0
    for _, width in cuts:
        for zl_, c_, zh_ in itertools.product(range(2), range(2), range(2)):
            made.append((low if c_ == 0 else high)[zh_, zl_, :, at : at + width])
        at += width
    return jnp.concatenate(made, axis=1).astype(F32)


QKV_CUTS = ((0, QCOLS), (H * HD, HD), ((H + KVH) * HD, HD))
FFN_CUTS = ((0, FCOLS), (FF, FCOLS))
WIDE = 512


def fold(v):
    return jnp.concatenate(
        [v[:, i : i + WIDE] for i in range(0, v.shape[1], WIDE)], axis=0
    )


def to_plane(u):
    return u.reshape(4, 2, 4, 64, u.shape[-1]).transpose(0, 2, 1, 3, 4)


def layer(
    tokens,
    segments,
    qkv_weight,
    out_weight,
    attn_gain,
    query_gain,
    key_gain,
    ffn_weight,
    down_weight,
    ffn_gain,
    out_grad,
):
    zl, y, zh, x, c = [lax.axis_index(a) for a in AXES]
    z = 2 * zh + zl
    seqs = tokens.shape[0]
    rows = seqs * SEQ
    x_own = tokens.reshape(rows, D)
    g_own = out_grad.reshape(rows, D)

    gain_in = attn_gain.astype(F32)[:, None]
    gain_mid = ffn_gain.astype(F32)[:, None]
    qkv_mine = my_columns(
        (qkv_weight.astype(F32) * gain_in).astype(BF), QKV_CUTS, zl, zh, c
    ).reshape(128, CCOLS)
    halves = jnp.concatenate(
        [out_weight.reshape(2, 16, D), down_weight.reshape(2, 48, D)], axis=1
    )
    rows_mine = send(halves[0], spread_rows(0)) + send(halves[1], spread_rows(1))
    attn_pack = jnp.concatenate([qkv_mine, fold(rows_mine[:16])], axis=0)
    attn_all = lax.all_gather(attn_pack, ("y", "x"), axis=0, tiled=False)
    ffn_mine = my_columns(
        (ffn_weight.astype(F32) * gain_mid).astype(BF), FFN_CUTS, zl, zh, c
    ).reshape(128, 2 * FCOLS)
    ffn_pack = jnp.concatenate([fold(ffn_mine), fold(rows_mine[16:])], axis=0)
    ffn_all = lax.all_gather(ffn_pack, ("y", "x"), axis=0, tiled=False)

    w_qkv = (
        attn_all[:, :128]
        .reshape(4, 4, 2, 64, WIDE)
        .transpose(0, 2, 1, 3, 4)
        .reshape(D, CCOLS)
    )
    w_out = (
        attn_all[:, 128:].reshape(16, 4, 16, WIDE).transpose(0, 2, 1, 3).reshape(QCOLS, D)
    )
    w_ffn = (
        ffn_all[:, :384]
        .reshape(4, 4, 3, 2, 64, WIDE)
        .transpose(0, 3, 1, 4, 2, 5)
        .reshape(D, 2 * FCOLS)
    )
    w_down = (
        ffn_all[:, 384:].reshape(16, 4, 48, WIDE).transpose(0, 2, 1, 3).reshape(FCOLS, D)
    )

    f = ((y * 2 + zh) * 4 + x) * 2 + c
    spots = jnp.stack([query_gain, key_gain]).astype(F32)
    mine = lax.dynamic_update_slice(jnp.zeros((2, HD), F32), spots, (0, 2 * f))
    note = jnp.concatenate([segments.reshape(1, rows).astype(F32), mine], axis=0)
    note = jnp.stack(ring(note, "z"))
    note = jnp.concatenate([note, send(note, step("c", 1))], axis=0)
    docs = note[:, 0].reshape(-1)
    near = jnp.where(zl == 0, note[3] + note[7], note[1] + note[5])
    gains = (note[0] + note[4] + near)[1:]
    gains = sum(ring(gains, "x"))
    gains = sum(ring(gains, "y"))
    gains = jnp.pad(gains, ((0, 6), (0, 0)))
    total = docs.shape[0]
    docs = docs + 8.0 * (jnp.arange(total) // SEQ).astype(F32)
    dcol = docs.reshape(total, 1)
    drow = docs.reshape(total // BLOCK, 1, BLOCK)
    cos, sin = tables()

    x_all = gather_group(x_own)
    z_in, qkv, mixed, part = call_forward(x_all, w_qkv, w_out, dcol, drow, cos, sin, gains)
    hidden = x_own.astype(F32) + sum_group(part, rows)
    r_mid = root(hidden)
    z_mid_own = hidden * r_mid
    z_mid = gather_group(z_mid_own.astype(BF))
    g_all = gather_group(g_own)
    gate_up = plain(z_mid, w_ffn)
    gate, up = gate_up[:, :FCOLS], gate_up[:, FCOLS:]
    g_active = last(g_all, w_down)
    sig = jax.nn.sigmoid(gate)
    active = (gate * sig * up).astype(BF)
    g_gate = (g_active * up * sig * (1.0 + gate * (1.0 - sig))).astype(BF)
    g_up = (g_active * gate * sig).astype(BF)
    g_gate_up = jnp.concatenate([g_gate, g_up], axis=1)

    eg = sum_group(last(g_gate_up, w_ffn).astype(BF), rows)
    g_hidden = g_own.astype(F32) + r_mid * (
        eg - z_mid_own * jnp.mean(eg * z_mid_own, axis=-1, keepdims=True)
    )
    result = hidden + sum_group(plain(active, w_down).astype(BF), rows)

    u_ffn = first(z_mid, g_gate_up).astype(BF)
    u_down = first(active, g_all).astype(BF)
    ffn_sum = jnp.concatenate(
        [
            to_plane(u_ffn)
            .reshape(16, 128, 3, WIDE)
            .transpose(0, 2, 1, 3)
            .reshape(16, 384, WIDE),
            u_down.reshape(16, 48, 4, WIDE).transpose(0, 2, 1, 3).reshape(16, 192, WIDE),
        ],
        axis=1,
    )
    ffn_sum = lax.psum_scatter(
        ffn_sum.reshape(16 * 576, WIDE), ("y", "x"), scatter_dimension=0, tiled=True
    )

    g_low = gather_group(g_hidden.astype(BF))
    g_qkv, part, gain_part = call_backward(
        g_low, qkv, w_qkv, w_out, dcol, drow, cos, sin, gains
    )
    eg = sum_group(part, rows)
    x_f32 = x_own.astype(F32)
    r_in = root(x_f32)
    z_own = x_f32 * r_in
    g_tokens = g_hidden + r_in * (
        eg - z_own * jnp.mean(eg * z_own, axis=-1, keepdims=True)
    )

    u_qkv = first(z_in, g_qkv).astype(BF)
    u_out = first(mixed, g_low).astype(BF)
    attn_sum = jnp.concatenate(
        [
            to_plane(u_qkv).reshape(16, 128, WIDE),
            u_out.reshape(16, 16, 4, WIDE).transpose(0, 2, 1, 3).reshape(16, 64, WIDE),
        ],
        axis=1,
    )
    attn_sum = lax.psum_scatter(
        attn_sum.reshape(16 * 192, WIDE), ("y", "x"), scatter_dimension=0, tiled=True
    )

    u_qkv = own_rows(attn_sum[:128].reshape(2, 2, 32, CCOLS), QKV_CUTS, 4096, zl, zh, c)
    u_ffn = own_rows(
        ffn_sum[:384]
        .reshape(3, 128, WIDE)
        .transpose(1, 0, 2)
        .reshape(2, 2, 32, 2 * FCOLS),
        FFN_CUTS,
        2 * FF,
        zl,
        zh,
        c,
    )
    rows_sum = jnp.concatenate(
        [
            attn_sum[128:].reshape(4, 16, WIDE).transpose(1, 0, 2).reshape(16, D),
            ffn_sum[384:].reshape(4, 48, WIDE).transpose(1, 0, 2).reshape(48, D),
        ],
        axis=0,
    )
    halves = jnp.stack(
        [send(rows_sum, collect_rows(0)), send(rows_sum, collect_rows(1))]
    )
    halves = halves + send(halves, share_rows)
    d_out = halves[:, :16].reshape(32, D).astype(F32)
    d_down = halves[:, 16:].reshape(96, D).astype(F32)

    gain_sum = gain_part[:2]
    for axis in ("c", "z", "x", "y"):
        if axis == "c":
            gain_sum = gain_sum + send(gain_sum, step("c", 1))
        else:
            gain_sum = sum(ring(gain_sum, axis))
    gain_own = lax.dynamic_slice(gain_sum, (0, 2 * f), (2, 2))

    return (
        result.astype(BF).reshape(seqs, SEQ, D),
        g_tokens.reshape(seqs, SEQ, D),
        u_qkv * gain_in,
        d_out,
        jnp.sum(u_qkv * qkv_weight.astype(F32), axis=1),
        gain_own[0],
        gain_own[1],
        u_ffn * gain_mid,
        d_down,
        jnp.sum(u_ffn * ffn_weight.astype(F32), axis=1),
    )


def solution(mesh):
    fine = Mesh(mesh.devices.reshape([SIZES[a] for a in AXES]), AXES)
    batch = AXES
    shard = ("y", "zh", "x", "c")
    matrix = P(shard, None)
    vector = P(shard)
    return jax.shard_map(
        layer,
        mesh=fine,
        in_specs=(
            P(batch, None, None),
            P(batch, None),
            matrix,
            matrix,
            vector,
            vector,
            vector,
            matrix,
            matrix,
            vector,
            P(batch, None, None),
        ),
        out_specs=(
            P(batch, None, None),
            P(batch, None, None),
            matrix,
            matrix,
            vector,
            vector,
            vector,
            matrix,
            matrix,
            vector,
        ),
        check_vma=False,
    )
```

```python
import functools
import itertools

import jax
import jax.numpy as jnp
import numpy as np
from jax import lax
from jax.experimental import pallas as pl
from jax.experimental.pallas import tpu as pltpu
from jax.sharding import Mesh
from jax.sharding import PartitionSpec as P

D = 2048
H = 16
KVH = 8
HD = 128
FF = 6144
SEQ = 64
RANKS = 8
OWN = 128
GROUP = 1024
WIDE = 512
HALF = 256
ATTN_ROWS = 208
WITH_DOCS = D + 128
FFN_ROWS = 576
QCOLS = 2 * HD
CCOLS = 4 * HD
FCOLS = FF // RANKS
STEP = 256
SUB = 128

EPS = 1e-06
NEG = -1e30
BASE = 1000000.0
SCALE = HD**-0.5
BF = jnp.bfloat16
F32 = jnp.float32

AXES = ("zl", "y", "zh", "x", "c")
SIZES = {"zl": 2, "y": 4, "zh": 2, "x": 4, "c": 2}


def place(d):
    i = 0
    for a in AXES:
        i = i * SIZES[a] + d[a]
    return i


def pairs(move):
    found = []
    for t in itertools.product(*[range(SIZES[a]) for a in AXES]):
        d = dict(zip(AXES, t))
        e = move(dict(d))
        if e is not None:
            found.append((place(d), place(e)))
    return found


def step(axis, by):
    def move(d):
        if axis == "z":
            z = (d["zh"] * 2 + d["zl"] + by) % 4
            d["zh"], d["zl"] = z // 2, z % 2
        else:
            d[axis] = (d[axis] + by) % SIZES[axis]
        return d

    return move


def send(v, move):
    return lax.ppermute(v, AXES, pairs(move))


def partner(d):
    d["zl"], d["zh"] = 1 - d["zl"], 1 - d["zh"]
    return d


def spread_rows(d):
    return {
        "zl": d["y"] // 2,
        "y": d["x"],
        "zh": d["zh"],
        "x": 2 * d["c"] + (d["zl"] ^ (d["y"] // 2)),
        "c": d["y"] % 2,
    }


def collect_rows(flip):
    def move(d):
        return {
            "zl": d["zl"] ^ (d["x"] % 2) ^ flip,
            "y": 2 * d["zl"] + d["c"],
            "zh": d["zh"],
            "x": d["y"],
            "c": d["x"] // 2,
        }

    return move


def ring(v, axis):
    return [
        v,
        send(v, step(axis, -1)),
        send(v, step(axis, 2)),
        send(v, step(axis, 1)),
    ]


def back(parts, axis):
    return [
        parts[0],
        send(parts[1], step(axis, 1)),
        send(parts[2], step(axis, 2)),
        send(parts[3], step(axis, -1)),
    ]


def relay(v):
    half = v.shape[0] // 2
    before, behind = send(v, step("z", 1)), send(v, step("z", -1))
    low = send(before[:half], step("z", 1))
    high = send(behind[half:], step("z", -1))
    return [v, behind, low, high, before]


def both_cores(same):
    return [send(b, step("c", 1)) for b in same] + same


def all_at_once(same):
    return [send(jnp.concatenate(same, axis=0), step("c", 1))] + same


def gather_group(v):
    return both_cores(relay(v))


def sum_group(other, same, after=()):
    got = send(other, step("c", 1))
    out = call_join(same, got, after)
    return back(out, "z"), out[1]


def later(v, after):
    return v + sum(a[:1, :1] * 0 for a in after)


def last(a, b):
    return lax.dot_general(a, b, (((1,), (1,)), ((), ())), preferred_element_type=F32)


def first(a, b):
    return lax.dot_general(a, b, (((0,), (0,)), ((), ())), preferred_element_type=F32)


def plain(a, b):
    return jnp.dot(a, b, preferred_element_type=F32)


def root(v):
    return lax.rsqrt(jnp.mean(v * v, axis=-1, keepdims=True) + EPS)


ANY = pl.BlockSpec(memory_space=pltpu.HBM)


def whole(*shape):
    return pl.BlockSpec(
        shape, lambda *i: (0,) * len(shape), pipeline_mode=pl.Buffered(1)
    )


def out_whole(*shape):
    return pl.BlockSpec(shape, lambda *i: (0,) * len(shape))


STEPS = GROUP // STEP


def rows_of(width, step=STEP):
    return pl.BlockSpec((step, width), lambda i, *_: (i, 0))


def other_rows(width, step=STEP):
    last_one = GROUP // step // 2 - 1
    return pl.BlockSpec((step, width), lambda i, *_: (jnp.minimum(i, last_one), 0))


def same_rows(width, step=STEP):
    half = GROUP // step // 2
    return pl.BlockSpec((step, width), lambda i, *_: (jnp.maximum(i - half, 0), 0))


def far(*values):
    return [pltpu.with_memory_space_constraint(v, pltpu.HBM) for v in values]


def away(shape, dtype=BF):
    return pltpu.HBM(shape, dtype)


def made(shape, dtype=BF):
    return jax.ShapeDtypeStruct(shape, dtype)


def params(mib):
    return pltpu.CompilerParams(
        dimension_semantics=("arbitrary",), vmem_limit_bytes=mib * 1024 * 1024
    )


def cost(flops, moved, weight=1 / 64):
    return pl.CostEstimate(
        flops=int(flops * weight), bytes_accessed=int(moved * weight), transcendentals=0
    )


def to_plane(v):
    low = lax.broadcasted_iota(jnp.int32, (v.shape[0], 128), 1) < 64
    tiles = []
    for y, x in itertools.product(range(4), range(4)):
        at = y * 512 + (x // 2) * 128
        a, b = v[:, at : at + 128], v[:, at + 256 : at + 384]
        if x % 2 == 0:
            tiles.append(jnp.where(low, a, pltpu.roll(b, 64, 1)))
        else:
            tiles.append(jnp.where(low, pltpu.roll(a, 64, 1), b))
    return jnp.concatenate(tiles, axis=1)


def from_plane(v):
    low = lax.broadcasted_iota(jnp.int32, (v.shape[0], 128), 1) < 64
    tiles = []
    for y, zh, pair in itertools.product(range(4), range(2), range(2)):
        at = y * 512 + pair * 256
        a, b = v[:, at : at + 128], v[:, at + 128 : at + 256]
        if zh == 0:
            tiles.append(jnp.where(low, a, pltpu.roll(b, 64, 1)))
        else:
            tiles.append(jnp.where(low, pltpu.roll(a, 64, 1), b))
    return jnp.concatenate(tiles, axis=1)


def same_place(n):
    return lax.broadcasted_iota(jnp.int32, (n, n), 0) == lax.broadcasted_iota(
        jnp.int32, (n, n), 1
    )


def column(row):
    n = row.shape[1]
    return jnp.sum(jnp.where(same_place(n), row, 0.0), axis=1, keepdims=True)


def row_of(col):
    n = col.shape[0]
    return jnp.sum(jnp.where(same_place(n), col, 0.0), axis=0, keepdims=True)


def own_norm(x, doc, z):
    v = x[...].astype(F32)
    z[:, :D] = to_plane(v * root(v)).astype(BF)
    col = column(doc[...].astype(F32))
    z[:, D:] = jnp.broadcast_to(col, (OWN, 128)).astype(BF)


def call_own_norm(x, doc):
    return pl.pallas_call(
        own_norm,
        grid=(1,),
        in_specs=[out_whole(OWN, D), out_whole(1, OWN)],
        out_specs=out_whole(OWN, WITH_DOCS),
        out_shape=made((OWN, WITH_DOCS)),
        compiler_params=params(8),
        cost_estimate=cost(1 << 20, 1 << 20),
    )(x, doc)


def added(parts):
    total = parts[0][...].astype(F32)
    for p in parts[1:]:
        total = total + p[...].astype(F32)
    return total


def own_middle(x, *refs):
    parts, (hidden, z) = refs[:4], refs[-2:]
    v = x[...].astype(F32) + added(parts)
    hidden[...] = v
    z[...] = to_plane(v * root(v)).astype(BF)


def own_back(count, v, g, *refs):
    parts, outs = refs[:4], refs[-count:]
    eg = from_plane(added(parts))
    v = v[...].astype(F32)
    r = root(v)
    z = v * r
    total = g[...].astype(F32) + r * (eg - z * jnp.mean(eg * z, axis=-1, keepdims=True))
    outs[0][...] = total
    if len(outs) > 1:
        outs[1][...] = total.astype(BF)


def own_result(hidden, *refs):
    parts, out = refs[:4], refs[-1]
    out[...] = (hidden[...] + added(parts)).astype(BF)


def call_own(body, ins, outs, after=(), weight=1):
    return pl.pallas_call(
        body,
        grid=(1,),
        in_specs=[out_whole(OWN, D) for _ in ins] + [ANY] * len(after),
        out_specs=[out_whole(OWN, D) for _ in outs],
        out_shape=[made((OWN, D), t) for t in outs],
        compiler_params=params(12),
        cost_estimate=cost(weight << 20, 4 << 20, 1),
    )(*ins, *far(*after))


def join(*refs):
    same, got, outs = refs[0], refs[1], refs[-4:]
    for j in range(4):
        r = slice(j * OWN, (j + 1) * OWN)
        total = same[r].astype(F32) + got[r].astype(F32)
        outs[j][...] = total.astype(outs[j].dtype)


def call_join(same, got, after=()):
    return pl.pallas_call(
        join,
        grid=(1,),
        in_specs=[out_whole(4 * OWN, D)] * 2 + [ANY] * len(after),
        out_specs=[out_whole(OWN, D)] * 4,
        out_shape=[made((OWN, D), F32)] + [made((OWN, D))] * 3,
        compiler_params=params(12),
        cost_estimate=cost(1 << 20, 6 << 20),
    )(same, got, *far(*after))


def block_copy(blocks, held, sems, j):
    start = sum(b.shape[0] for b in blocks[:j])
    return pltpu.make_async_copy(
        blocks[j], held.at[pl.ds(start, blocks[j].shape[0])], sems.at[j]
    )


def bring(blocks, held, sems, step=STEP):
    i = pl.program_id(0)

    @pl.when(i == 0)
    def _():
        for j in range(len(blocks)):
            block_copy(blocks, held, sems, j).start()

    for n in range(GROUP // step):

        @pl.when(i == n)
        def _():
            start = 0
            for j, b in enumerate(blocks):
                if start // step == n:
                    block_copy(blocks, held, sems, j).wait()
                start += b.shape[0]

    return held[pl.ds(pl.multiple_of(i * step, step), step), :]


def put_part(at, value, other, same, half=STEPS // 2):
    i = pl.program_id(0)

    @pl.when(i < half)
    def _():
        other[:, at : at + value.shape[1]] = value

    @pl.when(i >= half)
    def _():
        same[:, at : at + value.shape[1]] = value


def rotate(v, cos, sin):
    return v * cos + pltpu.roll(v, HD // 2, 1) * sin


def unrotate(v, cos, sin):
    return v * cos + pltpu.roll(v * sin, HD // 2, 1)


def scores_of(query, key, keep):
    s = last(query, key) * SCALE
    s = jnp.where(keep, s, NEG)
    p = jnp.exp(s - jnp.max(s, axis=-1, keepdims=True))
    return p / jnp.sum(p, axis=-1, keepdims=True)


def keep_mask(doc):
    shape = (SUB, SUB)
    a = lax.broadcasted_iota(jnp.int32, shape, 0)
    b = lax.broadcasted_iota(jnp.int32, shape, 1)
    keep = (doc == doc.T) & (b <= a) & ((b >= SEQ) == (a >= SEQ))
    return jnp.concatenate([keep, keep], axis=0)


def gains_of(w):
    return jnp.sum(w[...].astype(F32), axis=0)


def heads_of(qkv, gains, cos, sin):
    q0, q1, k = qkv[:, :HD], qkv[:, HD:QCOLS], qkv[:, QCOLS : QCOLS + HD]
    gq, gk = gains[0:1], gains[1:2]
    r0, r1, rk = root(q0), root(q1), root(k)
    z0, z1, zk = q0 * r0, q1 * r1, k * rk
    a0 = rotate(z0 * gq, cos, sin).astype(BF)
    a1 = rotate(z1 * gq, cos, sin).astype(BF)
    ak = rotate(zk * gk, cos, sin).astype(BF)
    val = qkv[:, QCOLS + HD :].astype(BF)
    return (r0, r1, rk), (z0, z1, zk), (a0, a1, ak), val


def qkv_matrix(w):
    return w[:, :128, :].reshape(D, CCOLS)


def out_matrix(w, b):
    return w[:, 128 + 16 * b : 144 + 16 * b, :].reshape(QCOLS, WIDE)


ATTN = pl.BlockSpec((16, 192, WIDE), lambda *i: (0, 0, 0), pipeline_mode=pl.Buffered(1))
HEADS = pl.BlockSpec((16, 16, HD), lambda *i: (0, 12, 0), pipeline_mode=pl.Buffered(1))


def attn_forward(*refs):
    blocks, (w_in, heads, cos, sin) = refs[:6], refs[6:10]
    z_out, doc_out, qkv_out, mix_out, other, same, held, sems = refs[-8:]
    rows = bring(blocks, held, sems, 512)
    z, doc = rows[:, :D], rows[:, D:]
    z_out[...] = z
    doc_out[...] = doc
    doc = doc.astype(F32)
    w = w_in[...]
    qkv = plain(z, qkv_matrix(w))
    qkv_out[...] = qkv
    _, _, (a0, a1, ak), val = heads_of(qkv, gains_of(heads), cos[...], sin[...])
    for s in range(512 // SUB):
        r = slice(s * SUB, (s + 1) * SUB)
        p = scores_of(jnp.concatenate([a0[r], a1[r]], axis=0), ak[r], keep_mask(doc[r]))
        o = plain(p.astype(BF), val[r])
        mix_out[r, :HD] = o[:SUB].astype(BF)
        mix_out[r, HD:] = o[SUB:].astype(BF)
    for b in range(4):
        put_part(b * WIDE, plain(mix_out[...], out_matrix(w, b)).astype(BF), other, same, 1)


def norm_back(r, z, gain, e):
    eg = e * gain
    return r * (eg - z * jnp.mean(eg * z, axis=-1, keepdims=True)), jnp.sum(
        e * z, axis=0, keepdims=True
    )


def attn_backward(*refs):
    blocks = refs[:10]
    qkv_in, w_in, heads, doc, cos, sin = refs[10:16]
    g_out, gqkv_out, other, same, gain_out, held, sems = refs[-7:]
    i = pl.program_id(0)
    g = bring(blocks, held, sems)
    g_out[...] = g
    w = w_in[...]
    gm = last(g[:, :WIDE], out_matrix(w, 0))
    for b in range(1, 4):
        gm = gm + last(g[:, b * WIDE : (b + 1) * WIDE], out_matrix(w, b))
    gm = gm.astype(BF)
    gain = gains_of(heads)
    c, s_ = cos[...], sin[...]
    (r0, r1, rk), (z0, z1, zk), (a0, a1, ak), val = heads_of(qkv_in[...], gain, c, s_)
    d0, d1, dk, dv = [], [], [], []
    for s in range(STEP // SUB):
        r = slice(s * SUB, (s + 1) * SUB)
        keep = keep_mask(doc[r, :].astype(F32))
        q = jnp.concatenate([a0[r], a1[r]], axis=0)
        do = jnp.concatenate([gm[r, :HD], gm[r, HD:]], axis=0)
        p = scores_of(q, ak[r], keep)
        dp = last(do, val[r])
        ds = (p * (dp - jnp.sum(p * dp, axis=-1, keepdims=True))).astype(BF)
        dq = plain(ds, ak[r]) * SCALE
        d0.append(dq[:SUB])
        d1.append(dq[SUB:])
        dk.append(first(ds, q) * SCALE)
        dv.append(first(p.astype(BF), do))
    d0, d1, dk, dv = [jnp.concatenate(v, axis=0) for v in (d0, d1, dk, dv)]
    g0, t0 = norm_back(r0, z0, gain[0:1], unrotate(d0, c, s_))
    g1, t1 = norm_back(r1, z1, gain[0:1], unrotate(d1, c, s_))
    gk, tk = norm_back(rk, zk, gain[1:2], unrotate(dk, c, s_))
    gqkv_out[:, :HD] = g0.astype(BF)
    gqkv_out[:, HD:QCOLS] = g1.astype(BF)
    gqkv_out[:, QCOLS : QCOLS + HD] = gk.astype(BF)
    gqkv_out[:, QCOLS + HD :] = dv.astype(BF)
    put_part(0, last(gqkv_out[...], qkv_matrix(w)).astype(BF), other, same)

    @pl.when(i == 0)
    def _():
        gain_out[...] = jnp.zeros_like(gain_out)

    gain_out[0:1] += t0 + t1
    gain_out[1:2] += tk


TABLES = [whole(STEP, HD), whole(STEP, HD)]


def held_rows(width):
    return [pltpu.VMEM((GROUP, width), BF), pltpu.SemaphoreType.DMA((10,))]


def call_forward(blocks, w, cos, sin, after):
    return pl.pallas_call(
        attn_forward,
        grid=(2,),
        in_specs=[ANY] * 6 + [ATTN, HEADS] + [whole(512, HD)] * 2 + [ANY] * len(after),
        out_specs=[
            rows_of(D, 512),
            rows_of(HD, 512),
            rows_of(CCOLS, 512),
            rows_of(QCOLS, 512),
            other_rows(D, 512),
            same_rows(D, 512),
        ],
        scratch_shapes=held_rows(WITH_DOCS),
        out_shape=[
            away((GROUP, D)),
            away((GROUP, HD)),
            away((GROUP, CCOLS), F32),
            away((GROUP, QCOLS)),
            made((GROUP // 2, D)),
            made((GROUP // 2, D)),
        ],
        compiler_params=params(36),
        cost_estimate=cost(2 * GROUP * D * (CCOLS + QCOLS) * 2, 20 << 20),
    )(*far(*blocks, w, w), jnp.tile(cos, (2, 1)), jnp.tile(sin, (2, 1)), *far(*after))


def call_backward(blocks, qkv, w, doc, cos, sin, after):
    return pl.pallas_call(
        attn_backward,
        grid=(STEPS,),
        in_specs=[ANY] * 10
        + [rows_of(CCOLS), ATTN, HEADS, rows_of(HD)]
        + TABLES
        + [ANY] * len(after),
        out_specs=[
            rows_of(D),
            rows_of(CCOLS),
            other_rows(D),
            same_rows(D),
            out_whole(8, HD),
        ],
        scratch_shapes=held_rows(D),
        out_shape=[
            made((GROUP, D)),
            made((GROUP, CCOLS)),
            made((GROUP // 2, D)),
            made((GROUP // 2, D)),
            made((8, HD), F32),
        ],
        compiler_params=params(28),
        cost_estimate=cost(2 * GROUP * D * (CCOLS + QCOLS) * 2, 20 << 20, 20),
    )(*far(*blocks), qkv, *far(w, w), doc, cos, sin, *far(*after))


def ffn_matrix(w, j):
    return w[:, 128 * j : 128 * (j + 1), :].reshape(D, WIDE)


def down_matrix(w, b):
    return w[:, 48 * b : 48 * b + 48, :].reshape(FCOLS, WIDE)


DOWN = pl.BlockSpec((16, 192, WIDE), lambda *i: (0, 2, 0), pipeline_mode=pl.Buffered(1))


def ffn_both(*refs):
    blocks, out_blocks, w_in = refs[:10], refs[10:16], refs[16]
    z_out, g_out, act_out, ggu_out, other, same = refs[17:23]
    held, sems, kept, marks, w, down, w_sems, wide = refs[23:]
    i = pl.program_id(0)

    def w_copy(j):
        if j < 3:
            src = w_in.at[:, pl.ds(128 * j, 128), :]
            dst = w.at[:, :, pl.ds(WIDE * j, WIDE)]
        else:
            src = w_in.at[:, pl.ds(384 + 48 * (j - 3), 48), :]
            dst = down.at[:, :, pl.ds(WIDE * (j - 3), WIDE)]
        return pltpu.make_async_copy(src, dst, w_sems.at[j])

    def arrived(*found):
        @pl.when(i == 0)
        def _():
            for j in found:
                w_copy(j).wait()

    @pl.when(i == 0)
    def _():
        for j in range(7):
            w_copy(j).start()

    z = bring(blocks, held, sems)
    g = bring(out_blocks, kept, marks)
    z_out[...] = z
    g_out[...] = g
    for j in range(3):
        arrived(j)
        cols = slice(j * WIDE, (j + 1) * WIDE)
        wide[:, cols] = plain(z, w[:, :, cols].reshape(D, WIDE))
    arrived(3, 4, 5, 6)
    for n in range(3):
        a, b = slice(n * 256, (n + 1) * 256), slice(FCOLS + n * 256, FCOLS + (n + 1) * 256)
        ga = last(g, down[...].reshape(FCOLS, D)[a])
        gate, up = wide[:, a], wide[:, b]
        sig = jax.nn.sigmoid(gate)
        silu = gate * sig
        act_out[:, a] = (silu * up).astype(BF)
        ggu_out[:, a] = (ga * up * sig * (1.0 + gate * (1.0 - sig))).astype(BF)
        ggu_out[:, b] = (ga * silu).astype(BF)
    for y in range(4):
        part = last(ggu_out[...], w[4 * y : 4 * y + 4].reshape(WIDE, 2 * FCOLS))
        put_part(y * WIDE, part.astype(BF), other, same)


def call_ffn(blocks, out_blocks, w):
    return pl.pallas_call(
        ffn_both,
        grid=(STEPS,),
        in_specs=[ANY] * 17,
        out_specs=[
            rows_of(D),
            rows_of(D),
            rows_of(FCOLS),
            rows_of(2 * FCOLS),
            other_rows(D),
            same_rows(D),
        ],
        scratch_shapes=held_rows(D) * 2
        + [
            pltpu.VMEM((16, 128, 2 * FCOLS), BF),
            pltpu.VMEM((16, 48, D), BF),
            pltpu.SemaphoreType.DMA((7,)),
            pltpu.VMEM((STEP, 2 * FCOLS), F32),
        ],
        out_shape=[
            away((GROUP, D)),
            away((GROUP, D)),
            away((GROUP, FCOLS)),
            away((GROUP, 2 * FCOLS)),
            made((GROUP // 2, D)),
            made((GROUP // 2, D)),
        ],
        compiler_params=params(44),
        cost_estimate=cost(8 * GROUP * D * FCOLS, 30 << 20),
    )(*far(*blocks, *out_blocks, w))


def ffn_grads(z, ggu, act, g, *refs):
    out, down = refs[-2:]
    y = pl.program_id(0)

    @pl.when(y == 0)
    def _():
        down[...] = first(act[...], g[...]).astype(BF)

    for j in range(3):
        u = first(z[...], ggu[:, j * WIDE : (j + 1) * WIDE]).astype(BF)
        for x in range(4):
            out[x, 128 * j : 128 * (j + 1), :] = u[128 * x : 128 * (x + 1)]
    for x in range(4):
        r = pl.ds(pl.multiple_of(192 * y + 48 * x, 16), 48)
        for b in range(4):
            out[x, 384 + 48 * b : 432 + 48 * b, :] = down[r, b * WIDE : (b + 1) * WIDE]


def call_ffn_grads(z, ggu, act, g, after):
    return pl.pallas_call(
        ffn_grads,
        grid=(4,),
        in_specs=[
            pl.BlockSpec((GROUP, WIDE), lambda y: (0, y)),
            whole(GROUP, 2 * FCOLS),
            whole(GROUP, FCOLS),
            whole(GROUP, D),
        ]
        + [ANY] * len(after),
        out_specs=pl.BlockSpec((4, FFN_ROWS, WIDE), lambda y: (y, 0, 0)),
        scratch_shapes=[pltpu.VMEM((FCOLS, D), BF)],
        out_shape=away((16, FFN_ROWS, WIDE)),
        compiler_params=params(32),
        cost_estimate=cost(6 * GROUP * D * FCOLS, 24 << 20, 20),
    )(*far(z, ggu, act, g, *after))


def ffn_result(act, w_in, *refs):
    other, same = refs[-2:]
    for b in range(4):
        put_part(
            b * WIDE, plain(act[...], down_matrix(w_in, b)).astype(BF), other, same
        )


def call_result(act, w, after):
    return pl.pallas_call(
        ffn_result,
        grid=(STEPS,),
        in_specs=[rows_of(FCOLS), DOWN] + [ANY] * len(after),
        out_specs=[other_rows(D), same_rows(D)],
        out_shape=[made((GROUP // 2, D)), made((GROUP // 2, D))],
        compiler_params=params(24),
        cost_estimate=cost(2 * GROUP * D * FCOLS, 16 << 20),
    )(*far(act, w, *after))


def attn_grads(z, gqkv, mixed, g, gain, *refs):
    out, os = refs[-2:]
    y = pl.program_id(0)

    @pl.when(y == 0)
    def _():
        os[...] = first(mixed[...], g[...]).astype(BF)

    us = first(z[...], gqkv[...]).astype(BF)
    extra = jnp.concatenate([gain[...], jnp.zeros((8, HD), F32)], axis=0).astype(BF)
    for x in range(4):
        r = pl.ds(pl.multiple_of(64 * y + 16 * x, 16), 16)
        out[x, :128, :] = us[128 * x : 128 * (x + 1)]
        for b in range(4):
            out[x, 128 + 16 * b : 144 + 16 * b, :] = os[r, b * WIDE : (b + 1) * WIDE]
        out[x, 192:, :HD] = extra
        out[x, 192:, HD:] = jnp.zeros((16, WIDE - HD), BF)


def call_attn_grads(z, gqkv, mixed, g, gain, after):
    return pl.pallas_call(
        attn_grads,
        grid=(4,),
        in_specs=[
            pl.BlockSpec((GROUP, WIDE), lambda y: (0, y)),
            whole(GROUP, CCOLS),
            whole(GROUP, QCOLS),
            whole(GROUP, D),
            whole(8, HD),
        ]
        + [ANY] * len(after),
        out_specs=pl.BlockSpec((4, ATTN_ROWS, WIDE), lambda y: (y, 0, 0)),
        scratch_shapes=[pltpu.VMEM((QCOLS, D), BF)],
        out_shape=away((16, ATTN_ROWS, WIDE)),
        compiler_params=params(24),
        cost_estimate=cost(2 * GROUP * D * (CCOLS + QCOLS), 16 << 20),
    )(z, gqkv, mixed, g, gain, *far(*after))


def pack_sums(attn, ffn, mine, rows):
    u = attn[0].astype(F32)
    for k in range(1, 16):
        u = u + attn[k].astype(F32)
    u = u.astype(BF)
    for zh, c in itertools.product(range(2), range(2)):
        r = 32 * (2 * zh + c)
        for zl in range(2):
            at = 4 * zl + 2 * zh + c
            mine[at, :, :WIDE] = u[r : r + 32]
            for j in range(3):
                mine[at, :, WIDE * (j + 1) : WIDE * (j + 2)] = ffn[
                    128 * j + r : 128 * j + r + 32
                ]
            mine[at, :16, 2048:] = u[192:, :HD]
            mine[at, 16:, 2048:] = jnp.zeros((16, HD), BF)
    for b in range(4):
        cols = slice(b * WIDE, (b + 1) * WIDE)
        rows[:16, cols] = u[128 + 16 * b : 144 + 16 * b]
        rows[16:, cols] = ffn[384 + 48 * b : 432 + 48 * b]


def call_pack_sums(attn, ffn):
    return pl.pallas_call(
        pack_sums,
        grid=(1,),
        in_specs=[out_whole(16, ATTN_ROWS, WIDE), out_whole(FFN_ROWS, WIDE)],
        out_specs=[out_whole(8, 32, 2048 + HD), out_whole(64, D)],
        out_shape=[away((8, 32, 2048 + HD)), made((64, D))],
        compiler_params=params(24),
        cost_estimate=cost(1 << 20, 4 << 20),
    )(*far(attn, ffn))


def own_columns(got, w_qkv, w_ffn, gain_in, gain_mid, d_qkv, d_ffn, d_in, d_mid, d_heads):
    for w, gain, out, d_gain, cuts, start in (
        (w_qkv, gain_in, d_qkv, d_in, QKV_CUTS, 0),
        (w_ffn, gain_mid, d_ffn, d_mid, FFN_CUTS, CCOLS),
    ):
        col = column(gain[...].astype(F32))
        total = jnp.zeros((32, 1), F32)
        for begin, width in cuts:
            for zl, c, zh in itertools.product(range(2), range(2), range(2)):
                at = begin + (4 * zl + 2 * c + zh) * width
                u = got[4 * zl + 2 * zh + c, :, start : start + width].astype(F32)
                out[:, at : at + width] = u * col
                total = total + jnp.sum(
                    u * w[:, at : at + width].astype(F32), axis=1, keepdims=True
                )
            start += width
        d_gain[...] = row_of(total)
    heads = got[0, :16, 2048:].astype(F32)
    for r in range(1, 8):
        heads = heads + got[r, :16, 2048:].astype(F32)
    d_heads[...] = heads


def call_own_columns(got, w_qkv, w_ffn, gain_in, gain_mid):
    shapes = [(32, 4096), (32, 2 * FF), (1, 32), (1, 32), (16, HD)]
    ins = (got, w_qkv, w_ffn, gain_in, gain_mid)
    return pl.pallas_call(
        own_columns,
        grid=(1,),
        in_specs=[out_whole(*v.shape) for v in ins],
        out_specs=[out_whole(*v) for v in shapes],
        out_shape=[made(v, F32) for v in shapes],
        compiler_params=params(24),
        cost_estimate=cost(1 << 20, 4 << 20),
    )(*ins)


def tables():
    half = HD // 2
    freq = BASE ** (-(np.arange(half, dtype=np.float64) * 2.0 / HD))
    angles = np.arange(SEQ, dtype=np.float64)[:, None] * freq
    cos = np.concatenate([np.cos(angles)] * 2, axis=-1)
    sin = np.concatenate([-np.sin(angles), np.sin(angles)], axis=-1)
    reps = (STEP // SEQ, 1)
    return np.tile(cos, reps).astype(np.float32), np.tile(sin, reps).astype(np.float32)


QKV_CUTS = ((0, QCOLS), (H * HD, HD), ((H + KVH) * HD, HD))
FFN_CUTS = ((0, FCOLS), (FF, FCOLS))
EXTRA = CCOLS + HD


def split_weights(at, w_qkv, w_ffn, gain_in, gain_mid, g_query, g_key, *outs):
    spot = lax.broadcasted_iota(jnp.int32, (1, HD), 1) - 2 * at[4]
    heads = [
        jnp.where(spot == 0, g[:, :1], jnp.where(spot == 1, g[:, 1:], 0.0))
        for g in (g_query[...].astype(F32), g_key[...].astype(F32))
    ]
    heads = jnp.concatenate(heads + [jnp.zeros((30, HD), F32)], axis=0).astype(BF)
    col_in = column(gain_in[...].astype(F32))
    col_mid = column(gain_mid[...].astype(F32))
    for n in range(4):
        attn, ffn = outs[n // 2].at[n % 2], outs[2 + n // 2].at[n % 2]
        for w, col, out, cuts in (
            (w_qkv, col_in, attn, QKV_CUTS),
            (w_ffn, col_mid, ffn, FFN_CUTS),
        ):
            start = 0
            for begin, width in cuts:
                from_ = pl.multiple_of(begin + at[n] * width, 128)
                part = w[:, pl.ds(from_, width)].astype(F32) * col
                out[:, start : start + width] = part.astype(BF)
                start += width
        attn[:, CCOLS:] = heads


def call_split_weights(at, w_qkv, w_ffn, gain_in, gain_mid, g_query, g_key):
    ins = (w_qkv, w_ffn, gain_in, gain_mid, g_query, g_key)
    shapes = [(2, 32, EXTRA)] * 2 + [(2, 32, 2 * FCOLS)] * 2
    return pl.pallas_call(
        split_weights,
        grid_spec=pltpu.PrefetchScalarGridSpec(
            num_scalar_prefetch=1,
            grid=(1,),
            in_specs=[out_whole(*v.shape) for v in ins],
            out_specs=[out_whole(*v) for v in shapes],
        ),
        out_shape=[made(v) for v in shapes],
        compiler_params=params(12),
        cost_estimate=cost(1 << 20, 2 << 20),
    )(at, *far(*ins))


def pack_first(at, near, got, far, rows, out):
    blocks = (near[0], got[0], far[0], far[1])
    for n, block in enumerate(blocks):
        zh, c = at[0] ^ (n // 2), at[1] ^ (n % 2)
        begin = pl.multiple_of(64 * zh + 32 * c, 32)
        out[pl.ds(begin, 32), :] = block[:, :CCOLS]
    for b in range(4):
        out[128 + 16 * b : 144 + 16 * b, :] = rows[:, b * WIDE : (b + 1) * WIDE]
    heads = sum(block[:16, CCOLS:].astype(F32) for block in blocks)
    out[192:, :HD] = heads.astype(BF)
    out[192:, HD:] = jnp.zeros((16, WIDE - HD), BF)


def pack_second(at, near, got, far, rows, *refs):
    out = refs[-1]
    for n, block in enumerate((near[0], got[0], far[0], far[1])):
        zh, c = at[0] ^ (n // 2), at[1] ^ (n % 2)
        for j in range(3):
            begin = pl.multiple_of(128 * j + 64 * zh + 32 * c, 32)
            out[pl.ds(begin, 32), :] = block[:, j * WIDE : (j + 1) * WIDE]
    for b in range(4):
        out[384 + 48 * b : 432 + 48 * b, :] = rows[:, b * WIDE : (b + 1) * WIDE]


def call_pack(body, at, total, *ins, after=()):
    return pl.pallas_call(
        body,
        grid_spec=pltpu.PrefetchScalarGridSpec(
            num_scalar_prefetch=1,
            grid=(1,),
            in_specs=[out_whole(*v.shape) for v in ins] + [ANY] * len(after),
            out_specs=out_whole(total, WIDE),
        ),
        out_shape=made((total, WIDE)),
        compiler_params=params(12),
        cost_estimate=cost(1 << 20, 2 << 20),
    )(at, *ins, *far(*after))


def fold(v):
    return jnp.concatenate(
        [v[:, i : i + WIDE] for i in range(0, v.shape[1], WIDE)], axis=0
    )


def layer(
    tokens,
    segments,
    qkv_weight,
    out_weight,
    attn_gain,
    query_gain,
    key_gain,
    ffn_weight,
    down_weight,
    ffn_gain,
    out_grad,
):
    zl, y, zh, x, c = [lax.axis_index(a) for a in AXES]
    seqs = tokens.shape[0]
    x_own = tokens.reshape(OWN, D)
    g_own = out_grad.reshape(OWN, D)
    cos, sin = tables()

    f = ((y * 2 + zh) * 4 + x) * 2 + c
    gain_in, gain_mid = attn_gain.reshape(1, 32), ffn_gain.reshape(1, 32)
    near, distant = 4 * zl + zh, 4 * (1 - zl) + (1 - zh)
    at = jnp.stack(
        [near + 2 * c, distant + 2 * c, near + 2 * (1 - c), distant + 2 * (1 - c), f]
    ).astype(jnp.int32)
    attn_keep, attn_give, ffn_keep, ffn_give = call_split_weights(
        at,
        qkv_weight,
        ffn_weight,
        gain_in,
        gain_mid,
        query_gain.reshape(1, 2),
        key_gain.reshape(1, 2),
    )
    attn_got = send(attn_give, step("c", 1))
    attn_far = send(jnp.stack([attn_keep[1], attn_got[1]]), partner)
    home = (y // 2) == zl
    here = jnp.stack([zh, c]).astype(jnp.int32)
    pack = call_pack(
        pack_first,
        here,
        ATTN_ROWS,
        attn_keep,
        attn_got,
        attn_far,
        give_rows(out_weight, home),
    )
    w_first = lax.all_gather(pack, ("y", "x"), axis=0, tiled=False)
    z_own = call_own_norm(x_own, segments.reshape(1, OWN))
    z_same, out_same = relay(z_own), relay(g_own)
    in_blocks = all_at_once(z_same)
    ffn_got = send(ffn_give, step("c", 1))
    ffn_far = send(jnp.stack([ffn_keep[1], ffn_got[1]]), partner)
    pack = call_pack(
        pack_second,
        here,
        FFN_ROWS,
        ffn_keep,
        ffn_got,
        ffn_far,
        give_rows(down_weight, home),
        after=in_blocks[:1] + out_same[1:],
    )
    w_second = lax.all_gather(pack, ("y", "x"), axis=0, tiled=False)

    out_blocks = all_at_once(out_same)
    z_in, doc, qkv, mixed, other, same = call_forward(
        in_blocks, w_first, cos, sin, out_same[1:]
    )
    parts, _ = sum_group(other, same)
    hidden, z_own = call_own(
        own_middle, [x_own] + parts, [F32, BF]
    )
    z_blocks = gather_group(z_own)
    z_mid, g_all, active, g_gate_up, other, same = call_ffn(
        z_blocks, out_blocks, w_second
    )

    parts, sent = sum_group(other, same)
    ffn_sum = call_ffn_grads(z_mid, g_gate_up, active, g_all, (sent,))
    g_hidden, g_low = call_own(
        functools.partial(own_back, 2),
        [hidden, g_own] + parts,
        [F32, BF],
        (ffn_sum,),
    )
    g_blocks = gather_group(g_low)
    g_low, g_qkv, other, same, gain_part = call_backward(
        g_blocks, qkv, w_first, doc, cos, sin, ()
    )
    parts, sent = sum_group(other, same)
    (g_tokens,) = call_own(
        functools.partial(own_back, 1), [x_own, g_hidden] + parts, [F32]
    )

    result_other, result_same = call_result(active, w_second, (sent,))
    result_parts, _ = sum_group(result_other, result_same, (parts[3],))
    (result,) = call_own(own_result, [hidden] + result_parts, [BF])

    ffn_sum = lax.psum_scatter(
        ffn_sum.reshape(16 * FFN_ROWS, WIDE), ("y", "x"), scatter_dimension=0, tiled=True
    )
    attn_sum = call_attn_grads(z_in, g_qkv, mixed, g_low, gain_part, (sent,))
    attn_sum = lax.all_to_all(attn_sum, ("y", "x"), 0, 0, tiled=True)
    mine, rows = call_pack_sums(attn_sum, ffn_sum)
    got = lax.all_to_all(mine, ("zl", "zh", "c"), 0, 0, tiled=True)
    d_qkv, d_ffn, d_in, d_mid, gain_sum = call_own_columns(
        got, qkv_weight, ffn_weight, gain_in, gain_mid
    )
    gain_own = lax.dynamic_slice(gain_sum, (0, 2 * f), (2, 2))
    low, high = take_rows(rows, home)
    d_out = jnp.concatenate([low[:16], high[:16]], axis=0).astype(F32)
    d_down = jnp.concatenate([low[16:], high[16:]], axis=0).astype(F32)

    return (
        result.reshape(seqs, SEQ, D),
        g_tokens.reshape(seqs, SEQ, D),
        d_qkv,
        d_out,
        d_in[0],
        gain_own[0],
        gain_own[1],
        d_ffn,
        d_down,
        d_mid[0],
    )


def give_rows(shard, home):
    half = shard.shape[0] // 2
    return send(jnp.where(home, shard[:half], shard[half:]), spread_rows)


def take_rows(v, home):
    a, b = send(v, collect_rows(0)), send(v, collect_rows(1))
    return jnp.where(home, a, b), jnp.where(home, b, a)


def solution(mesh):
    fine = Mesh(mesh.devices.reshape([SIZES[a] for a in AXES]), AXES)
    batch = AXES
    shard = ("y", "zh", "x", "c")
    matrix = P(shard, None)
    vector = P(shard)
    return jax.shard_map(
        layer,
        mesh=fine,
        in_specs=(
            P(batch, None, None),
            P(batch, None),
            matrix,
            matrix,
            vector,
            vector,
            vector,
            matrix,
            matrix,
            vector,
            P(batch, None, None),
        ),
        out_specs=(
            P(batch, None, None),
            P(batch, None, None),
            matrix,
            matrix,
            vector,
            vector,
            vector,
            matrix,
            matrix,
            vector,
        ),
        check_vma=False,
    )
```

```python
import functools
import itertools

import jax
import jax.numpy as jnp
import numpy as np
from jax import lax
from jax.experimental import pallas as pl
from jax.experimental.pallas import tpu as pltpu
from jax.sharding import Mesh
from jax.sharding import PartitionSpec as P

D = 2048
H = 16
KVH = 8
HD = 128
FF = 6144
SEQ = 64
RANKS = 8
OWN = 128
GROUP = 1024
WIDE = 512
HALF = 256
ATTN_ROWS = 208
WITH_DOCS = D + 128
FFN_ROWS = 576
QCOLS = 2 * HD
CCOLS = 4 * HD
FCOLS = FF // RANKS
STEP = 256
SUB = 128

EPS = 1e-06
NEG = -1e30
BASE = 1000000.0
SCALE = HD**-0.5
BF = jnp.bfloat16
F32 = jnp.float32

AXES = ("zl", "y", "zh", "x", "c")
SIZES = {"zl": 2, "y": 4, "zh": 2, "x": 4, "c": 2}


def place(d):
    i = 0
    for a in AXES:
        i = i * SIZES[a] + d[a]
    return i


def pairs(move):
    found = []
    for t in itertools.product(*[range(SIZES[a]) for a in AXES]):
        d = dict(zip(AXES, t))
        e = move(dict(d))
        if e is not None:
            found.append((place(d), place(e)))
    return found


def step(axis, by):
    def move(d):
        if axis == "z":
            z = (d["zh"] * 2 + d["zl"] + by) % 4
            d["zh"], d["zl"] = z // 2, z % 2
        else:
            d[axis] = (d[axis] + by) % SIZES[axis]
        return d

    return move


def send(v, move):
    return lax.ppermute(v, AXES, pairs(move))


def partner(d):
    d["zl"], d["zh"] = 1 - d["zl"], 1 - d["zh"]
    return d


def spread_rows(d):
    return {
        "zl": d["y"] // 2,
        "y": d["x"],
        "zh": d["zh"],
        "x": 2 * d["c"] + (d["zl"] ^ (d["y"] // 2)),
        "c": d["y"] % 2,
    }


def collect_rows(d):
    return {
        "zl": d["zl"] ^ (d["x"] % 2),
        "y": 2 * d["zl"] + d["c"],
        "zh": d["zh"],
        "x": d["y"],
        "c": d["x"] // 2,
    }


def other_plane(d):
    d["zl"] = 1 - d["zl"]
    return d


def ring(v, axis):
    return [
        v,
        send(v, step(axis, -1)),
        send(v, step(axis, 2)),
        send(v, step(axis, 1)),
    ]


def back(parts, axis):
    return [
        parts[0],
        send(parts[1], step(axis, 1)),
        send(parts[2], step(axis, 2)),
        send(parts[3], step(axis, -1)),
    ]


def relay(v):
    half = v.shape[0] // 2
    before, behind = send(v, step("z", 1)), send(v, step("z", -1))
    low = send(before[:half], step("z", 1))
    high = send(behind[half:], step("z", -1))
    return [v, behind, low, high, before]


def both_cores(same):
    return [send(b, step("c", 1)) for b in same] + same


def all_at_once(same):
    return [send(jnp.concatenate(same, axis=0), step("c", 1))] + same


def gather_group(v):
    return both_cores(relay(v))


def sum_group(other, same, after=()):
    got = send(other, step("c", 1))
    out = call_join(same, got, after)
    return back(out, "z"), out[1]


def sum_relay(other, same):
    got = send(other, step("c", 1))
    own, ahead, low, high, behind = call_join_halves(same, got)
    from_low, from_high = send(low, step("z", 1)), send(high, step("z", -1))
    ahead, behind = call_add_halves(ahead, from_low, behind, from_high)
    return [own, send(ahead, step("z", 1)), send(behind, step("z", -1))], low


def later(v, after):
    return v + sum(a[:1, :1] * 0 for a in after)


def last(a, b):
    return lax.dot_general(a, b, (((1,), (1,)), ((), ())), preferred_element_type=F32)


def first(a, b):
    return lax.dot_general(a, b, (((0,), (0,)), ((), ())), preferred_element_type=F32)


def plain(a, b):
    return jnp.dot(a, b, preferred_element_type=F32)


def root(v):
    return lax.rsqrt(jnp.mean(v * v, axis=-1, keepdims=True) + EPS)


ANY = pl.BlockSpec(memory_space=pltpu.HBM)


def whole(*shape):
    return pl.BlockSpec(
        shape, lambda *i: (0,) * len(shape), pipeline_mode=pl.Buffered(1)
    )


def out_whole(*shape):
    return pl.BlockSpec(shape, lambda *i: (0,) * len(shape))


STEPS = GROUP // STEP


def rows_of(width, step=STEP):
    return pl.BlockSpec((step, width), lambda i, *_: (i, 0))


def other_rows(width, step=STEP):
    last_one = GROUP // step // 2 - 1
    return pl.BlockSpec((step, width), lambda i, *_: (jnp.minimum(i, last_one), 0))


def same_rows(width, step=STEP):
    half = GROUP // step // 2
    return pl.BlockSpec((step, width), lambda i, *_: (jnp.maximum(i - half, 0), 0))


def far(*values):
    return [pltpu.with_memory_space_constraint(v, pltpu.HBM) for v in values]


def away(shape, dtype=BF):
    return pltpu.HBM(shape, dtype)


def made(shape, dtype=BF):
    return jax.ShapeDtypeStruct(shape, dtype)


def params(mib):
    return pltpu.CompilerParams(
        dimension_semantics=("arbitrary",), vmem_limit_bytes=mib * 1024 * 1024
    )


def cost(flops, moved, weight=1 / 64):
    return pl.CostEstimate(
        flops=int(flops * weight), bytes_accessed=int(moved * weight), transcendentals=0
    )


def to_plane(v):
    low = lax.broadcasted_iota(jnp.int32, (v.shape[0], 128), 1) < 64
    tiles = []
    for y, x in itertools.product(range(4), range(4)):
        at = y * 512 + (x // 2) * 128
        a, b = v[:, at : at + 128], v[:, at + 256 : at + 384]
        if x % 2 == 0:
            tiles.append(jnp.where(low, a, pltpu.roll(b, 64, 1)))
        else:
            tiles.append(jnp.where(low, pltpu.roll(a, 64, 1), b))
    return jnp.concatenate(tiles, axis=1)


def from_plane(v):
    low = lax.broadcasted_iota(jnp.int32, (v.shape[0], 128), 1) < 64
    tiles = []
    for y, zh, pair in itertools.product(range(4), range(2), range(2)):
        at = y * 512 + pair * 256
        a, b = v[:, at : at + 128], v[:, at + 128 : at + 256]
        if zh == 0:
            tiles.append(jnp.where(low, a, pltpu.roll(b, 64, 1)))
        else:
            tiles.append(jnp.where(low, pltpu.roll(a, 64, 1), b))
    return jnp.concatenate(tiles, axis=1)


def same_place(n):
    return lax.broadcasted_iota(jnp.int32, (n, n), 0) == lax.broadcasted_iota(
        jnp.int32, (n, n), 1
    )


def column(row):
    n = row.shape[1]
    return jnp.sum(jnp.where(same_place(n), row, 0.0), axis=1, keepdims=True)


def row_of(col):
    n = col.shape[0]
    return jnp.sum(jnp.where(same_place(n), col, 0.0), axis=0, keepdims=True)


def own_norm(x, doc, z):
    v = x[...].astype(F32)
    z[:, :D] = to_plane(v * root(v)).astype(BF)
    col = column(doc[...].astype(F32))
    z[:, D:] = jnp.broadcast_to(col, (OWN, 128)).astype(BF)


def call_own_norm(x, doc):
    return pl.pallas_call(
        own_norm,
        grid=(1,),
        in_specs=[out_whole(OWN, D), out_whole(1, OWN)],
        out_specs=out_whole(OWN, WITH_DOCS),
        out_shape=made((OWN, WITH_DOCS)),
        compiler_params=params(8),
        cost_estimate=cost(1 << 20, 1 << 20),
    )(x, doc)


def added(parts):
    total = parts[0][...].astype(F32)
    for p in parts[1:]:
        total = total + p[...].astype(F32)
    return total


def own_middle(x, *refs):
    parts, (hidden, z) = refs[:3], refs[-2:]
    v = x[...].astype(F32) + added(parts)
    hidden[...] = v
    z[...] = to_plane(v * root(v)).astype(BF)


def own_back(count, pieces, v, g, *refs):
    parts, outs = refs[:pieces], refs[-count:]
    eg = from_plane(added(parts))
    v = v[...].astype(F32)
    r = root(v)
    z = v * r
    total = g[...].astype(F32) + r * (eg - z * jnp.mean(eg * z, axis=-1, keepdims=True))
    outs[0][...] = total
    if len(outs) > 1:
        outs[1][...] = total.astype(BF)


def own_result(hidden, *refs):
    parts, out = refs[:3], refs[-1]
    out[...] = (hidden[...] + added(parts)).astype(BF)


def call_own(body, ins, outs, after=(), weight=1):
    return pl.pallas_call(
        body,
        grid=(1,),
        in_specs=[out_whole(OWN, D) for _ in ins] + [ANY] * len(after),
        out_specs=[out_whole(OWN, D) for _ in outs],
        out_shape=[made((OWN, D), t) for t in outs],
        compiler_params=params(12),
        cost_estimate=cost(weight << 20, 4 << 20, 1),
    )(*ins, *far(*after))


def join(*refs):
    same, got, outs = refs[0], refs[1], refs[-4:]
    for j in range(4):
        r = slice(j * OWN, (j + 1) * OWN)
        total = same[r].astype(F32) + got[r].astype(F32)
        outs[j][...] = total.astype(outs[j].dtype)


def call_join(same, got, after=()):
    return pl.pallas_call(
        join,
        grid=(1,),
        in_specs=[out_whole(4 * OWN, D)] * 2 + [ANY] * len(after),
        out_specs=[out_whole(OWN, D)] * 4,
        out_shape=[made((OWN, D), F32)] + [made((OWN, D))] * 3,
        compiler_params=params(12),
        cost_estimate=cost(1 << 20, 6 << 20),
    )(same, got, *far(*after))


def join_halves(same, got, own, ahead, low, high, behind):
    at = 0
    for out in (own, ahead, low, high, behind):
        r = slice(at, at + out.shape[0])
        out[...] = (same[r].astype(F32) + got[r].astype(F32)).astype(out.dtype)
        at += out.shape[0]


def call_join_halves(same, got):
    shapes = [(OWN, F32), (OWN, F32), (OWN // 2, BF), (OWN // 2, BF), (OWN, F32)]
    return pl.pallas_call(
        join_halves,
        grid=(1,),
        in_specs=[out_whole(4 * OWN, D)] * 2,
        out_specs=[out_whole(n, D) for n, _ in shapes],
        out_shape=[made((n, D), t) for n, t in shapes],
        compiler_params=params(12),
        cost_estimate=cost(1 << 20, 6 << 20),
    )(same, got)


def add_halves(ahead, low, behind, high, to_ahead, to_behind):
    half = OWN // 2
    to_ahead[:half, :] = (ahead[:half] + low[...].astype(F32)).astype(BF)
    to_ahead[half:, :] = ahead[half:].astype(BF)
    to_behind[:half, :] = behind[:half].astype(BF)
    to_behind[half:, :] = (behind[half:] + high[...].astype(F32)).astype(BF)


def call_add_halves(ahead, low, behind, high):
    ins = (ahead, low, behind, high)
    return pl.pallas_call(
        add_halves,
        grid=(1,),
        in_specs=[out_whole(*v.shape) for v in ins],
        out_specs=[out_whole(OWN, D)] * 2,
        out_shape=[made((OWN, D))] * 2,
        compiler_params=params(12),
        cost_estimate=cost(1 << 20, 2 << 20),
    )(*ins)


def block_copy(blocks, held, sems, j):
    start = sum(b.shape[0] for b in blocks[:j])
    return pltpu.make_async_copy(
        blocks[j], held.at[pl.ds(start, blocks[j].shape[0])], sems.at[j]
    )


def bring(blocks, held, sems, step=STEP):
    i = pl.program_id(0)

    @pl.when(i == 0)
    def _():
        for j in range(len(blocks)):
            block_copy(blocks, held, sems, j).start()

    for n in range(GROUP // step):

        @pl.when(i == n)
        def _():
            start = 0
            for j, b in enumerate(blocks):
                if start // step == n:
                    block_copy(blocks, held, sems, j).wait()
                start += b.shape[0]

    return held[pl.ds(pl.multiple_of(i * step, step), step), :]


def put_part(at, value, other, same, half=STEPS // 2):
    i = pl.program_id(0)

    @pl.when(i < half)
    def _():
        other[:, at : at + value.shape[1]] = value

    @pl.when(i >= half)
    def _():
        same[:, at : at + value.shape[1]] = value


def rotate(v, cos, sin):
    return v * cos + pltpu.roll(v, HD // 2, 1) * sin


def unrotate(v, cos, sin):
    return v * cos + pltpu.roll(v * sin, HD // 2, 1)


def scores_of(query, key, keep):
    s = last(query, key) * SCALE
    s = jnp.where(keep, s, NEG)
    p = jnp.exp(s - jnp.max(s, axis=-1, keepdims=True))
    return p / jnp.sum(p, axis=-1, keepdims=True)


def keep_mask(doc):
    shape = (SUB, SUB)
    a = lax.broadcasted_iota(jnp.int32, shape, 0)
    b = lax.broadcasted_iota(jnp.int32, shape, 1)
    keep = (doc == doc.T) & (b <= a) & ((b >= SEQ) == (a >= SEQ))
    return jnp.concatenate([keep, keep], axis=0)


def gains_of(w):
    return jnp.sum(w[...].astype(F32), axis=0)


def heads_of(qkv, gains, cos, sin):
    q0, q1, k = qkv[:, :HD], qkv[:, HD:QCOLS], qkv[:, QCOLS : QCOLS + HD]
    gq, gk = gains[0:1], gains[1:2]
    r0, r1, rk = root(q0), root(q1), root(k)
    z0, z1, zk = q0 * r0, q1 * r1, k * rk
    a0 = rotate(z0 * gq, cos, sin).astype(BF)
    a1 = rotate(z1 * gq, cos, sin).astype(BF)
    ak = rotate(zk * gk, cos, sin).astype(BF)
    val = qkv[:, QCOLS + HD :].astype(BF)
    return (r0, r1, rk), (z0, z1, zk), (a0, a1, ak), val


def qkv_matrix(w):
    return w[:, :128, :].reshape(D, CCOLS)


def out_matrix(w, b):
    return w[:, 128 + 16 * b : 144 + 16 * b, :].reshape(QCOLS, WIDE)


ATTN = pl.BlockSpec((16, 192, WIDE), lambda *i: (0, 0, 0), pipeline_mode=pl.Buffered(1))
HEADS = pl.BlockSpec((16, 16, HD), lambda *i: (0, 12, 0), pipeline_mode=pl.Buffered(1))


def attn_forward(*refs):
    blocks, (w_in, heads, cos, sin) = refs[:6], refs[6:10]
    z_out, doc_out, qkv_out, mix_out, other, same, held, sems = refs[-8:]
    rows = bring(blocks, held, sems, 512)
    z, doc = rows[:, :D], rows[:, D:]
    z_out[...] = z
    doc_out[...] = doc
    doc = doc.astype(F32)
    w = w_in[...]
    qkv = plain(z, qkv_matrix(w))
    qkv_out[...] = qkv
    _, _, (a0, a1, ak), val = heads_of(qkv, gains_of(heads), cos[...], sin[...])
    for s in range(512 // SUB):
        r = slice(s * SUB, (s + 1) * SUB)
        p = scores_of(jnp.concatenate([a0[r], a1[r]], axis=0), ak[r], keep_mask(doc[r]))
        o = plain(p.astype(BF), val[r])
        mix_out[r, :HD] = o[:SUB].astype(BF)
        mix_out[r, HD:] = o[SUB:].astype(BF)
    for b in range(4):
        put_part(b * WIDE, plain(mix_out[...], out_matrix(w, b)).astype(BF), other, same, 1)


def norm_back(r, z, gain, e):
    eg = e * gain
    return r * (eg - z * jnp.mean(eg * z, axis=-1, keepdims=True)), jnp.sum(
        e * z, axis=0, keepdims=True
    )


def attn_backward(*refs):
    blocks = refs[:10]
    qkv_in, w_in, heads, doc, cos, sin = refs[10:16]
    g_out, gqkv_out, other, same, gain_out, held, sems = refs[-7:]
    i = pl.program_id(0)
    g = bring(blocks, held, sems)
    g_out[...] = g
    w = w_in[...]
    gm = last(g[:, :WIDE], out_matrix(w, 0))
    for b in range(1, 4):
        gm = gm + last(g[:, b * WIDE : (b + 1) * WIDE], out_matrix(w, b))
    gm = gm.astype(BF)
    gain = gains_of(heads)
    c, s_ = cos[...], sin[...]
    (r0, r1, rk), (z0, z1, zk), (a0, a1, ak), val = heads_of(qkv_in[...], gain, c, s_)
    d0, d1, dk, dv = [], [], [], []
    for s in range(STEP // SUB):
        r = slice(s * SUB, (s + 1) * SUB)
        keep = keep_mask(doc[r, :].astype(F32))
        q = jnp.concatenate([a0[r], a1[r]], axis=0)
        do = jnp.concatenate([gm[r, :HD], gm[r, HD:]], axis=0)
        p = scores_of(q, ak[r], keep)
        dp = last(do, val[r])
        ds = (p * (dp - jnp.sum(p * dp, axis=-1, keepdims=True))).astype(BF)
        dq = plain(ds, ak[r]) * SCALE
        d0.append(dq[:SUB])
        d1.append(dq[SUB:])
        dk.append(first(ds, q) * SCALE)
        dv.append(first(p.astype(BF), do))
    d0, d1, dk, dv = [jnp.concatenate(v, axis=0) for v in (d0, d1, dk, dv)]
    g0, t0 = norm_back(r0, z0, gain[0:1], unrotate(d0, c, s_))
    g1, t1 = norm_back(r1, z1, gain[0:1], unrotate(d1, c, s_))
    gk, tk = norm_back(rk, zk, gain[1:2], unrotate(dk, c, s_))
    gqkv_out[:, :HD] = g0.astype(BF)
    gqkv_out[:, HD:QCOLS] = g1.astype(BF)
    gqkv_out[:, QCOLS : QCOLS + HD] = gk.astype(BF)
    gqkv_out[:, QCOLS + HD :] = dv.astype(BF)
    put_part(0, last(gqkv_out[...], qkv_matrix(w)).astype(BF), other, same)

    @pl.when(i == 0)
    def _():
        gain_out[...] = jnp.zeros_like(gain_out)

    gain_out[0:1] += t0 + t1
    gain_out[1:2] += tk


TABLES = [whole(STEP, HD), whole(STEP, HD)]


def held_rows(width):
    return [pltpu.VMEM((GROUP, width), BF), pltpu.SemaphoreType.DMA((10,))]


def call_forward(blocks, w, cos, sin, after):
    return pl.pallas_call(
        attn_forward,
        grid=(2,),
        in_specs=[ANY] * 6 + [ATTN, HEADS] + [whole(512, HD)] * 2 + [ANY] * len(after),
        out_specs=[
            rows_of(D, 512),
            rows_of(HD, 512),
            rows_of(CCOLS, 512),
            rows_of(QCOLS, 512),
            other_rows(D, 512),
            same_rows(D, 512),
        ],
        scratch_shapes=held_rows(WITH_DOCS),
        out_shape=[
            away((GROUP, D)),
            away((GROUP, HD)),
            away((GROUP, CCOLS), F32),
            away((GROUP, QCOLS)),
            made((GROUP // 2, D)),
            made((GROUP // 2, D)),
        ],
        compiler_params=params(36),
        cost_estimate=cost(2 * GROUP * D * (CCOLS + QCOLS) * 2, 20 << 20),
    )(*far(*blocks, w, w), jnp.tile(cos, (2, 1)), jnp.tile(sin, (2, 1)), *far(*after))


def call_backward(blocks, qkv, w, doc, cos, sin, after):
    return pl.pallas_call(
        attn_backward,
        grid=(STEPS,),
        in_specs=[ANY] * 10
        + [rows_of(CCOLS), ATTN, HEADS, rows_of(HD)]
        + TABLES
        + [ANY] * len(after),
        out_specs=[
            rows_of(D),
            rows_of(CCOLS),
            other_rows(D),
            same_rows(D),
            out_whole(8, HD),
        ],
        scratch_shapes=held_rows(D),
        out_shape=[
            made((GROUP, D)),
            made((GROUP, CCOLS)),
            made((GROUP // 2, D)),
            made((GROUP // 2, D)),
            made((8, HD), F32),
        ],
        compiler_params=params(28),
        cost_estimate=cost(2 * GROUP * D * (CCOLS + QCOLS) * 2, 20 << 20, 5),
    )(*far(*blocks), qkv, *far(w, w), doc, cos, sin, *far(*after))


def ffn_matrix(w, j):
    return w[:, 128 * j : 128 * (j + 1), :].reshape(D, WIDE)


def down_matrix(w, b):
    return w[:, 48 * b : 48 * b + 48, :].reshape(FCOLS, WIDE)


DOWN = pl.BlockSpec((16, 192, WIDE), lambda *i: (0, 2, 0), pipeline_mode=pl.Buffered(1))


def ffn_both(*refs):
    blocks, out_blocks, w_in = refs[:10], refs[10:16], refs[16]
    z_out, g_out, act_out, ggu_out, other, same = refs[17:23]
    held, sems, kept, marks, w, down, w_sems, wide = refs[23:]
    i = pl.program_id(0)

    def w_copy(j):
        if j < 3:
            src = w_in.at[:, pl.ds(128 * j, 128), :]
            dst = w.at[:, :, pl.ds(WIDE * j, WIDE)]
        else:
            src = w_in.at[:, pl.ds(384 + 48 * (j - 3), 48), :]
            dst = down.at[:, :, pl.ds(WIDE * (j - 3), WIDE)]
        return pltpu.make_async_copy(src, dst, w_sems.at[j])

    def arrived(*found):
        @pl.when(i == 0)
        def _():
            for j in found:
                w_copy(j).wait()

    @pl.when(i == 0)
    def _():
        for j in range(7):
            w_copy(j).start()

    z = bring(blocks, held, sems)
    g = bring(out_blocks, kept, marks)
    z_out[...] = z
    g_out[...] = g
    for j in range(3):
        arrived(j)
        cols = slice(j * WIDE, (j + 1) * WIDE)
        wide[:, cols] = plain(z, w[:, :, cols].reshape(D, WIDE))
    arrived(3, 4, 5, 6)
    for n in range(3):
        a, b = slice(n * 256, (n + 1) * 256), slice(FCOLS + n * 256, FCOLS + (n + 1) * 256)
        ga = last(g, down[...].reshape(FCOLS, D)[a])
        gate, up = wide[:, a], wide[:, b]
        sig = jax.nn.sigmoid(gate)
        silu = gate * sig
        act_out[:, a] = (silu * up).astype(BF)
        ggu_out[:, a] = (ga * up * sig * (1.0 + gate * (1.0 - sig))).astype(BF)
        ggu_out[:, b] = (ga * silu).astype(BF)
    for y in range(4):
        part = last(ggu_out[...], w[4 * y : 4 * y + 4].reshape(WIDE, 2 * FCOLS))
        put_part(y * WIDE, part.astype(BF), other, same)


def call_ffn(blocks, out_blocks, w):
    return pl.pallas_call(
        ffn_both,
        grid=(STEPS,),
        in_specs=[ANY] * 17,
        out_specs=[
            rows_of(D),
            rows_of(D),
            rows_of(FCOLS),
            rows_of(2 * FCOLS),
            other_rows(D),
            same_rows(D),
        ],
        scratch_shapes=held_rows(D) * 2
        + [
            pltpu.VMEM((16, 128, 2 * FCOLS), BF),
            pltpu.VMEM((16, 48, D), BF),
            pltpu.SemaphoreType.DMA((7,)),
            pltpu.VMEM((STEP, 2 * FCOLS), F32),
        ],
        out_shape=[
            away((GROUP, D)),
            away((GROUP, D)),
            away((GROUP, FCOLS)),
            away((GROUP, 2 * FCOLS)),
            made((GROUP // 2, D)),
            made((GROUP // 2, D)),
        ],
        compiler_params=params(44),
        cost_estimate=cost(8 * GROUP * D * FCOLS, 30 << 20),
    )(*far(*blocks, *out_blocks, w))


def ffn_grads(z, ggu, act, g, *refs):
    out, down = refs[-2:]
    y = pl.program_id(0)

    @pl.when(y == 0)
    def _():
        down[...] = first(act[...], g[...]).astype(BF)

    for j in range(3):
        u = first(z[...], ggu[:, j * WIDE : (j + 1) * WIDE]).astype(BF)
        for x in range(4):
            out[x, 128 * j : 128 * (j + 1), :] = u[128 * x : 128 * (x + 1)]
    for x in range(4):
        r = pl.ds(pl.multiple_of(192 * y + 48 * x, 16), 48)
        for b in range(4):
            out[x, 384 + 48 * b : 432 + 48 * b, :] = down[r, b * WIDE : (b + 1) * WIDE]


def call_ffn_grads(z, ggu, act, g, after):
    return pl.pallas_call(
        ffn_grads,
        grid=(4,),
        in_specs=[
            pl.BlockSpec((GROUP, WIDE), lambda y: (0, y)),
            whole(GROUP, 2 * FCOLS),
            whole(GROUP, FCOLS),
            whole(GROUP, D),
        ]
        + [ANY] * len(after),
        out_specs=pl.BlockSpec((4, FFN_ROWS, WIDE), lambda y: (y, 0, 0)),
        scratch_shapes=[pltpu.VMEM((FCOLS, D), BF)],
        out_shape=away((16, FFN_ROWS, WIDE)),
        compiler_params=params(32),
        cost_estimate=cost(6 * GROUP * D * FCOLS, 24 << 20, 20),
    )(*far(z, ggu, act, g, *after))


def ffn_result(act, w_in, *refs):
    other, same = refs[-2:]
    for b in range(4):
        put_part(
            b * WIDE, plain(act[...], down_matrix(w_in, b)).astype(BF), other, same
        )


def call_result(act, w, after):
    return pl.pallas_call(
        ffn_result,
        grid=(STEPS,),
        in_specs=[rows_of(FCOLS), DOWN] + [ANY] * len(after),
        out_specs=[other_rows(D), same_rows(D)],
        out_shape=[made((GROUP // 2, D)), made((GROUP // 2, D))],
        compiler_params=params(24),
        cost_estimate=cost(2 * GROUP * D * FCOLS, 16 << 20),
    )(*far(act, w, *after))


def attn_grads(z, gqkv, mixed, g, gain, *refs):
    out, os = refs[-2:]
    y = pl.program_id(0)

    @pl.when(y == 0)
    def _():
        os[...] = first(mixed[...], g[...]).astype(BF)

    us = first(z[...], gqkv[...]).astype(BF)
    extra = jnp.concatenate([gain[...], jnp.zeros((8, HD), F32)], axis=0).astype(BF)
    for x in range(4):
        r = pl.ds(pl.multiple_of(64 * y + 16 * x, 16), 16)
        out[x, :128, :] = us[128 * x : 128 * (x + 1)]
        for b in range(4):
            out[x, 128 + 16 * b : 144 + 16 * b, :] = os[r, b * WIDE : (b + 1) * WIDE]
        out[x, 192:, :HD] = extra
        out[x, 192:, HD:] = jnp.zeros((16, WIDE - HD), BF)


def call_attn_grads(z, gqkv, mixed, g, gain, after):
    return pl.pallas_call(
        attn_grads,
        grid=(4,),
        in_specs=[
            pl.BlockSpec((GROUP, WIDE), lambda y: (0, y)),
            whole(GROUP, CCOLS),
            whole(GROUP, QCOLS),
            whole(GROUP, D),
            whole(8, HD),
        ]
        + [ANY] * len(after),
        out_specs=pl.BlockSpec((4, ATTN_ROWS, WIDE), lambda y: (y, 0, 0)),
        scratch_shapes=[pltpu.VMEM((QCOLS, D), BF)],
        out_shape=away((16, ATTN_ROWS, WIDE)),
        compiler_params=params(24),
        cost_estimate=cost(2 * GROUP * D * (CCOLS + QCOLS), 16 << 20),
    )(z, gqkv, mixed, g, gain, *far(*after))


def pack_sums(attn, ffn, *refs):
    mine, rows = refs[-2:]
    u = attn[0].astype(F32)
    for k in range(1, 16):
        u = u + attn[k].astype(F32)
    u = u.astype(BF)
    for zh, c in itertools.product(range(2), range(2)):
        r = 32 * (2 * zh + c)
        for zl in range(2):
            at = 4 * zl + 2 * zh + c
            mine[at, :, :WIDE] = u[r : r + 32]
            for j in range(3):
                mine[at, :, WIDE * (j + 1) : WIDE * (j + 2)] = ffn[
                    128 * j + r : 128 * j + r + 32
                ]
            mine[at, :16, 2048:] = u[192:, :HD]
            mine[at, 16:, 2048:] = jnp.zeros((16, HD), BF)
    for b in range(4):
        cols = slice(b * WIDE, (b + 1) * WIDE)
        rows[:16, cols] = u[128 + 16 * b : 144 + 16 * b]
        rows[16:, cols] = ffn[384 + 48 * b : 432 + 48 * b]


def call_pack_sums(attn, ffn, after):
    return pl.pallas_call(
        pack_sums,
        grid=(1,),
        in_specs=[out_whole(16, ATTN_ROWS, WIDE), out_whole(FFN_ROWS, WIDE)]
        + [ANY] * len(after),
        out_specs=[out_whole(8, 32, 2048 + HD), out_whole(64, D)],
        out_shape=[away((8, 32, 2048 + HD)), made((64, D))],
        compiler_params=params(24),
        cost_estimate=cost(1 << 20, 4 << 20),
    )(*far(attn, ffn, *after))


def own_columns(got, w_qkv, w_ffn, gain_in, gain_mid, d_qkv, d_ffn, d_in, d_mid, d_heads):
    for w, gain, out, d_gain, cuts, start in (
        (w_qkv, gain_in, d_qkv, d_in, QKV_CUTS, 0),
        (w_ffn, gain_mid, d_ffn, d_mid, FFN_CUTS, CCOLS),
    ):
        col = column(gain[...].astype(F32))
        total = jnp.zeros((32, 1), F32)
        for begin, width in cuts:
            for zl, c, zh in itertools.product(range(2), range(2), range(2)):
                at = begin + (4 * zl + 2 * c + zh) * width
                u = got[4 * zl + 2 * zh + c, :, start : start + width].astype(F32)
                out[:, at : at + width] = u * col
                total = total + jnp.sum(
                    u * w[:, at : at + width].astype(F32), axis=1, keepdims=True
                )
            start += width
        d_gain[...] = row_of(total)
    heads = got[0, :16, 2048:].astype(F32)
    for r in range(1, 8):
        heads = heads + got[r, :16, 2048:].astype(F32)
    d_heads[...] = heads


def call_own_columns(got, w_qkv, w_ffn, gain_in, gain_mid):
    shapes = [(32, 4096), (32, 2 * FF), (1, 32), (1, 32), (16, HD)]
    ins = (got, w_qkv, w_ffn, gain_in, gain_mid)
    return pl.pallas_call(
        own_columns,
        grid=(1,),
        in_specs=[out_whole(*v.shape) for v in ins],
        out_specs=[out_whole(*v) for v in shapes],
        out_shape=[made(v, F32) for v in shapes],
        compiler_params=params(24),
        cost_estimate=cost(1 << 20, 4 << 20),
    )(*ins)


def own_row_blocks(home, a, b, *refs):
    d_out, d_down = refs[-2:]
    for n in range(2):
        part = jnp.where(home[0] == 1 - n, a[...], b[...]).astype(F32)
        d_out[16 * n : 16 * (n + 1), :] = part[:16]
        d_down[48 * n : 48 * (n + 1), :] = part[16:]


def call_own_row_blocks(home, a, b, after):
    shapes = [(32, D), (96, D)]
    return pl.pallas_call(
        own_row_blocks,
        grid_spec=pltpu.PrefetchScalarGridSpec(
            num_scalar_prefetch=1,
            grid=(1,),
            in_specs=[out_whole(64, D)] * 2 + [ANY] * len(after),
            out_specs=[out_whole(*v) for v in shapes],
        ),
        out_shape=[made(v, F32) for v in shapes],
        compiler_params=params(8),
        cost_estimate=cost(1 << 20, 1 << 20),
    )(home, a, b, *far(*after))


def tables():
    half = HD // 2
    freq = BASE ** (-(np.arange(half, dtype=np.float64) * 2.0 / HD))
    angles = np.arange(SEQ, dtype=np.float64)[:, None] * freq
    cos = np.concatenate([np.cos(angles)] * 2, axis=-1)
    sin = np.concatenate([-np.sin(angles), np.sin(angles)], axis=-1)
    reps = (STEP // SEQ, 1)
    return np.tile(cos, reps).astype(np.float32), np.tile(sin, reps).astype(np.float32)


QKV_CUTS = ((0, QCOLS), (H * HD, HD), ((H + KVH) * HD, HD))
FFN_CUTS = ((0, FCOLS), (FF, FCOLS))
EXTRA = CCOLS + HD


def split_weights(at, w_qkv, w_ffn, gain_in, gain_mid, g_query, g_key, *outs):
    spot = lax.broadcasted_iota(jnp.int32, (1, HD), 1) - 2 * at[4]
    heads = [
        jnp.where(spot == 0, g[:, :1], jnp.where(spot == 1, g[:, 1:], 0.0))
        for g in (g_query[...].astype(F32), g_key[...].astype(F32))
    ]
    heads = jnp.concatenate(heads + [jnp.zeros((30, HD), F32)], axis=0).astype(BF)
    col_in = column(gain_in[...].astype(F32))
    col_mid = column(gain_mid[...].astype(F32))
    for n in range(4):
        attn, ffn = outs[n // 2].at[n % 2], outs[2 + n // 2].at[n % 2]
        for w, col, out, cuts in (
            (w_qkv, col_in, attn, QKV_CUTS),
            (w_ffn, col_mid, ffn, FFN_CUTS),
        ):
            start = 0
            for begin, width in cuts:
                from_ = pl.multiple_of(begin + at[n] * width, 128)
                part = w[:, pl.ds(from_, width)].astype(F32) * col
                out[:, start : start + width] = part.astype(BF)
                start += width
        attn[:, CCOLS:] = heads


def call_split_weights(at, w_qkv, w_ffn, gain_in, gain_mid, g_query, g_key):
    ins = (w_qkv, w_ffn, gain_in, gain_mid, g_query, g_key)
    shapes = [(2, 32, EXTRA)] * 2 + [(2, 32, 2 * FCOLS)] * 2
    return pl.pallas_call(
        split_weights,
        grid_spec=pltpu.PrefetchScalarGridSpec(
            num_scalar_prefetch=1,
            grid=(1,),
            in_specs=[out_whole(*v.shape) for v in ins],
            out_specs=[out_whole(*v) for v in shapes],
        ),
        out_shape=[made(v) for v in shapes],
        compiler_params=params(12),
        cost_estimate=cost(1 << 20, 2 << 20),
    )(at, *far(*ins))


def pack_first(at, near, got, far, rows, out):
    blocks = (near[0], got[0], far[0], far[1])
    for n, block in enumerate(blocks):
        zh, c = at[0] ^ (n // 2), at[1] ^ (n % 2)
        begin = pl.multiple_of(64 * zh + 32 * c, 32)
        out[pl.ds(begin, 32), :] = block[:, :CCOLS]
    for b in range(4):
        out[128 + 16 * b : 144 + 16 * b, :] = rows[:, b * WIDE : (b + 1) * WIDE]
    heads = sum(block[:16, CCOLS:].astype(F32) for block in blocks)
    out[192:, :HD] = heads.astype(BF)
    out[192:, HD:] = jnp.zeros((16, WIDE - HD), BF)


def pack_second(at, near, got, far, rows, *refs):
    out = refs[-1]
    for n, block in enumerate((near[0], got[0], far[0], far[1])):
        zh, c = at[0] ^ (n // 2), at[1] ^ (n % 2)
        for j in range(3):
            begin = pl.multiple_of(128 * j + 64 * zh + 32 * c, 32)
            out[pl.ds(begin, 32), :] = block[:, j * WIDE : (j + 1) * WIDE]
    for b in range(4):
        out[384 + 48 * b : 432 + 48 * b, :] = rows[:, b * WIDE : (b + 1) * WIDE]


def call_pack(body, at, total, *ins, after=()):
    return pl.pallas_call(
        body,
        grid_spec=pltpu.PrefetchScalarGridSpec(
            num_scalar_prefetch=1,
            grid=(1,),
            in_specs=[out_whole(*v.shape) for v in ins] + [ANY] * len(after),
            out_specs=out_whole(total, WIDE),
        ),
        out_shape=made((total, WIDE)),
        compiler_params=params(12),
        cost_estimate=cost(1 << 20, 2 << 20),
    )(at, *ins, *far(*after))


def fold(v):
    return jnp.concatenate(
        [v[:, i : i + WIDE] for i in range(0, v.shape[1], WIDE)], axis=0
    )


def layer(
    tokens,
    segments,
    qkv_weight,
    out_weight,
    attn_gain,
    query_gain,
    key_gain,
    ffn_weight,
    down_weight,
    ffn_gain,
    out_grad,
):
    zl, y, zh, x, c = [lax.axis_index(a) for a in AXES]
    seqs = tokens.shape[0]
    x_own = tokens.reshape(OWN, D)
    g_own = out_grad.reshape(OWN, D)
    cos, sin = tables()

    f = ((y * 2 + zh) * 4 + x) * 2 + c
    gain_in, gain_mid = attn_gain.reshape(1, 32), ffn_gain.reshape(1, 32)
    near, distant = 4 * zl + zh, 4 * (1 - zl) + (1 - zh)
    at = jnp.stack(
        [near + 2 * c, distant + 2 * c, near + 2 * (1 - c), distant + 2 * (1 - c), f]
    ).astype(jnp.int32)
    attn_keep, attn_give, ffn_keep, ffn_give = call_split_weights(
        at,
        qkv_weight,
        ffn_weight,
        gain_in,
        gain_mid,
        query_gain.reshape(1, 2),
        key_gain.reshape(1, 2),
    )
    attn_got = send(attn_give, step("c", 1))
    attn_far = send(jnp.stack([attn_keep[1], attn_got[1]]), partner)
    home = (y // 2) == zl
    here = jnp.stack([zh, c]).astype(jnp.int32)
    pack = call_pack(
        pack_first,
        here,
        ATTN_ROWS,
        attn_keep,
        attn_got,
        attn_far,
        give_rows(out_weight, home),
    )
    w_first = lax.all_gather(pack, ("y", "x"), axis=0, tiled=False)
    z_own = call_own_norm(x_own, segments.reshape(1, OWN))
    z_same, out_same = relay(z_own), relay(g_own)
    in_blocks = all_at_once(z_same)
    ffn_got = send(ffn_give, step("c", 1))
    ffn_far = send(jnp.stack([ffn_keep[1], ffn_got[1]]), partner)
    pack = call_pack(
        pack_second,
        here,
        FFN_ROWS,
        ffn_keep,
        ffn_got,
        ffn_far,
        give_rows(down_weight, home),
        after=z_same[1:] + out_same[1:],
    )
    w_second = lax.all_gather(pack, ("y", "x"), axis=0, tiled=False)

    out_blocks = all_at_once(out_same)
    z_in, doc, qkv, mixed, other, same = call_forward(
        in_blocks, w_first, cos, sin, out_same[1:]
    )
    parts, _ = sum_relay(other, same)
    hidden, z_own = call_own(
        own_middle, [x_own] + parts, [F32, BF]
    )
    z_blocks = gather_group(z_own)
    z_mid, g_all, active, g_gate_up, other, same = call_ffn(
        z_blocks, out_blocks, w_second
    )

    parts, sent = sum_group(other, same)
    ffn_sum = call_ffn_grads(z_mid, g_gate_up, active, g_all, (sent,))
    g_hidden, g_low = call_own(
        functools.partial(own_back, 2, 4),
        [hidden, g_own] + parts,
        [F32, BF],
        (ffn_sum,),
        250000,
    )
    g_blocks = gather_group(g_low)
    g_low, g_qkv, other, same, gain_part = call_backward(
        g_blocks, qkv, w_first, doc, cos, sin, ()
    )
    parts, sent = sum_relay(other, same)
    (g_tokens,) = call_own(
        functools.partial(own_back, 1, 3), [x_own, g_hidden] + parts, [F32]
    )
    result_other, result_same = call_result(active, w_second, (sent,))
    result_parts, _ = sum_relay(result_other, result_same)
    (result,) = call_own(own_result, [hidden] + result_parts, [BF])

    ffn_sum = lax.psum_scatter(
        ffn_sum.reshape(16 * FFN_ROWS, WIDE), ("y", "x"), scatter_dimension=0, tiled=True
    )
    attn_sum = call_attn_grads(z_in, g_qkv, mixed, g_low, gain_part, (sent,))
    attn_sum = lax.all_to_all(attn_sum, ("y", "x"), 0, 0, tiled=True)
    mine, rows = call_pack_sums(attn_sum, ffn_sum, (g_tokens, result))
    got = lax.all_to_all(mine, ("zl", "zh", "c"), 0, 0, tiled=True)
    d_qkv, d_ffn, d_in, d_mid, gain_sum = call_own_columns(
        got, qkv_weight, ffn_weight, gain_in, gain_mid
    )
    gain_own = lax.dynamic_slice(gain_sum, (0, 2 * f), (2, 2))
    d_out, d_down = call_own_row_blocks(
        home.astype(jnp.int32).reshape(1), *take_rows(rows), (d_in,)
    )

    return (
        result.reshape(seqs, SEQ, D),
        g_tokens.reshape(seqs, SEQ, D),
        d_qkv,
        d_out,
        d_in[0],
        gain_own[0],
        gain_own[1],
        d_ffn,
        d_down,
        d_mid[0],
    )


def give_rows(shard, home):
    half = shard.shape[0] // 2
    return send(jnp.where(home, shard[:half], shard[half:]), spread_rows)


def take_rows(v):
    mine = send(v, collect_rows)
    return mine, send(mine, other_plane)


def solution(mesh):
    fine = Mesh(mesh.devices.reshape([SIZES[a] for a in AXES]), AXES)
    batch = AXES
    shard = ("y", "zh", "x", "c")
    matrix = P(shard, None)
    vector = P(shard)
    return jax.shard_map(
        layer,
        mesh=fine,
        in_specs=(
            P(batch, None, None),
            P(batch, None),
            matrix,
            matrix,
            vector,
            vector,
            vector,
            matrix,
            matrix,
            vector,
            P(batch, None, None),
        ),
        out_specs=(
            P(batch, None, None),
            P(batch, None, None),
            matrix,
            matrix,
            vector,
            vector,
            vector,
            matrix,
            matrix,
            vector,
        ),
        check_vma=False,
    )
```

```python
import functools
import itertools

import jax
import jax.numpy as jnp
import numpy as np
from jax import lax
from jax.experimental import pallas as pl
from jax.experimental.pallas import tpu as pltpu
from jax.sharding import Mesh
from jax.sharding import PartitionSpec as P

D = 2048
H = 16
KVH = 8
HD = 128
FF = 6144
SEQ = 64
RANKS = 8
OWN = 128
GROUP = 1024
WIDE = 512
HALF = 256
ATTN_ROWS = 208
WITH_DOCS = D + 128
FFN_ROWS = 576
QCOLS = 2 * HD
CCOLS = 4 * HD
FCOLS = FF // RANKS
STEP = 256
SUB = 128

EPS = 1e-06
NEG = -1e30
BASE = 1000000.0
SCALE = HD**-0.5
BF = jnp.bfloat16
F32 = jnp.float32

AXES = ("zl", "y", "zh", "x", "c")
SIZES = {"zl": 2, "y": 4, "zh": 2, "x": 4, "c": 2}


def place(d):
    i = 0
    for a in AXES:
        i = i * SIZES[a] + d[a]
    return i


def pairs(move):
    found = []
    for t in itertools.product(*[range(SIZES[a]) for a in AXES]):
        d = dict(zip(AXES, t))
        e = move(dict(d))
        if e is not None:
            found.append((place(d), place(e)))
    return found


def step(axis, by):
    def move(d):
        if axis == "z":
            z = (d["zh"] * 2 + d["zl"] + by) % 4
            d["zh"], d["zl"] = z // 2, z % 2
        else:
            d[axis] = (d[axis] + by) % SIZES[axis]
        return d

    return move


def send(v, move):
    return lax.ppermute(v, AXES, pairs(move))


def partner(d):
    d["zl"], d["zh"] = 1 - d["zl"], 1 - d["zh"]
    return d


def spread_rows(d):
    return {
        "zl": d["y"] // 2,
        "y": d["x"],
        "zh": d["zh"],
        "x": 2 * d["c"] + (d["zl"] ^ (d["y"] // 2)),
        "c": d["y"] % 2,
    }


def collect_rows(d):
    return {
        "zl": d["zl"] ^ (d["x"] % 2),
        "y": 2 * d["zl"] + d["c"],
        "zh": d["zh"],
        "x": d["y"],
        "c": d["x"] // 2,
    }


def other_plane(d):
    d["zl"] = 1 - d["zl"]
    return d


def ring(v, axis):
    return [
        v,
        send(v, step(axis, -1)),
        send(v, step(axis, 2)),
        send(v, step(axis, 1)),
    ]


def back(parts, axis):
    return [
        parts[0],
        send(parts[1], step(axis, 1)),
        send(parts[2], step(axis, 2)),
        send(parts[3], step(axis, -1)),
    ]


def relay(v):
    half = v.shape[0] // 2
    before, behind = send(v, step("z", 1)), send(v, step("z", -1))
    low = send(before[:half], step("z", 1))
    high = send(behind[half:], step("z", -1))
    return [v, behind, low, high, before]


def both_cores(same):
    return [send(b, step("c", 1)) for b in same] + same


def all_at_once(same):
    return [send(jnp.concatenate(same, axis=0), step("c", 1))] + same


def gather_group(v):
    return both_cores(relay(v))


def sum_group(other, same, after=()):
    got = send(other, step("c", 1))
    out = call_join(same, got, after)
    return back(out, "z"), out[1]


def sum_relay(other, same):
    got = send(other, step("c", 1))
    own, ahead, low, high, behind = call_join_halves(same, got)
    from_low, from_high = send(low, step("z", 1)), send(high, step("z", -1))
    ahead, behind = call_add_halves(ahead, from_low, behind, from_high)
    return [own, send(ahead, step("z", 1)), send(behind, step("z", -1))], low


def later(v, after):
    return v + sum(a[:1, :1] * 0 for a in after)


def last(a, b):
    return lax.dot_general(a, b, (((1,), (1,)), ((), ())), preferred_element_type=F32)


def first(a, b):
    return lax.dot_general(a, b, (((0,), (0,)), ((), ())), preferred_element_type=F32)


def plain(a, b):
    return jnp.dot(a, b, preferred_element_type=F32)


def root(v):
    return lax.rsqrt(jnp.mean(v * v, axis=-1, keepdims=True) + EPS)


ANY = pl.BlockSpec(memory_space=pltpu.HBM)


def whole(*shape):
    return pl.BlockSpec(
        shape, lambda *i: (0,) * len(shape), pipeline_mode=pl.Buffered(1)
    )


def out_whole(*shape):
    return pl.BlockSpec(shape, lambda *i: (0,) * len(shape))


STEPS = GROUP // STEP


def rows_of(width, step=STEP):
    return pl.BlockSpec((step, width), lambda i, *_: (i, 0))


def other_rows(width, step=STEP):
    last_one = GROUP // step // 2 - 1
    return pl.BlockSpec((step, width), lambda i, *_: (jnp.minimum(i, last_one), 0))


def same_rows(width, step=STEP):
    half = GROUP // step // 2
    return pl.BlockSpec((step, width), lambda i, *_: (jnp.maximum(i - half, 0), 0))


def far(*values):
    return [pltpu.with_memory_space_constraint(v, pltpu.HBM) for v in values]


def away(shape, dtype=BF):
    return pltpu.HBM(shape, dtype)


def made(shape, dtype=BF):
    return jax.ShapeDtypeStruct(shape, dtype)


def params(mib):
    return pltpu.CompilerParams(
        dimension_semantics=("arbitrary",), vmem_limit_bytes=mib * 1024 * 1024
    )


def cost(flops, moved, weight=1 / 64):
    return pl.CostEstimate(
        flops=int(flops * weight), bytes_accessed=int(moved * weight), transcendentals=0
    )


def to_plane(v):
    low = lax.broadcasted_iota(jnp.int32, (v.shape[0], 128), 1) < 64
    tiles = []
    for y, x in itertools.product(range(4), range(4)):
        at = y * 512 + (x // 2) * 128
        a, b = v[:, at : at + 128], v[:, at + 256 : at + 384]
        if x % 2 == 0:
            tiles.append(jnp.where(low, a, pltpu.roll(b, 64, 1)))
        else:
            tiles.append(jnp.where(low, pltpu.roll(a, 64, 1), b))
    return jnp.concatenate(tiles, axis=1)


def from_plane(v):
    low = lax.broadcasted_iota(jnp.int32, (v.shape[0], 128), 1) < 64
    tiles = []
    for y, zh, pair in itertools.product(range(4), range(2), range(2)):
        at = y * 512 + pair * 256
        a, b = v[:, at : at + 128], v[:, at + 128 : at + 256]
        if zh == 0:
            tiles.append(jnp.where(low, a, pltpu.roll(b, 64, 1)))
        else:
            tiles.append(jnp.where(low, pltpu.roll(a, 64, 1), b))
    return jnp.concatenate(tiles, axis=1)


def same_place(n):
    return lax.broadcasted_iota(jnp.int32, (n, n), 0) == lax.broadcasted_iota(
        jnp.int32, (n, n), 1
    )


def column(row):
    n = row.shape[1]
    return jnp.sum(jnp.where(same_place(n), row, 0.0), axis=1, keepdims=True)


def row_of(col):
    n = col.shape[0]
    return jnp.sum(jnp.where(same_place(n), col, 0.0), axis=0, keepdims=True)


def own_norm(x, doc, z):
    v = x[...].astype(F32)
    z[:, :D] = to_plane(v * root(v)).astype(BF)
    col = column(doc[...].astype(F32))
    z[:, D:] = jnp.broadcast_to(col, (OWN, 128)).astype(BF)


def call_own_norm(x, doc):
    return pl.pallas_call(
        own_norm,
        grid=(1,),
        in_specs=[out_whole(OWN, D), out_whole(1, OWN)],
        out_specs=out_whole(OWN, WITH_DOCS),
        out_shape=made((OWN, WITH_DOCS)),
        compiler_params=params(8),
        cost_estimate=cost(1 << 20, 1 << 20),
    )(x, doc)


def added(parts):
    total = parts[0][...].astype(F32)
    for p in parts[1:]:
        total = total + p[...].astype(F32)
    return total


def own_middle(x, *refs):
    parts, (hidden, z) = refs[:3], refs[-2:]
    v = x[...].astype(F32) + added(parts)
    hidden[...] = v
    z[...] = to_plane(v * root(v)).astype(BF)


def own_back(count, pieces, v, g, *refs):
    parts, outs = refs[:pieces], refs[-count:]
    eg = from_plane(added(parts))
    v = v[...].astype(F32)
    r = root(v)
    z = v * r
    total = g[...].astype(F32) + r * (eg - z * jnp.mean(eg * z, axis=-1, keepdims=True))
    outs[0][...] = total
    if len(outs) > 1:
        outs[1][...] = total.astype(BF)


def own_result(hidden, *refs):
    parts, out = refs[:3], refs[-1]
    out[...] = (hidden[...] + added(parts)).astype(BF)


def call_own(body, ins, outs, after=(), weight=1):
    return pl.pallas_call(
        body,
        grid=(1,),
        in_specs=[out_whole(OWN, D) for _ in ins] + [ANY] * len(after),
        out_specs=[out_whole(OWN, D) for _ in outs],
        out_shape=[made((OWN, D), t) for t in outs],
        compiler_params=params(12),
        cost_estimate=cost(weight << 20, 4 << 20, 1),
    )(*ins, *far(*after))


def join(*refs):
    same, got, outs = refs[0], refs[1], refs[-4:]
    for j in range(4):
        r = slice(j * OWN, (j + 1) * OWN)
        total = same[r].astype(F32) + got[r].astype(F32)
        outs[j][...] = total.astype(outs[j].dtype)


def call_join(same, got, after=()):
    return pl.pallas_call(
        join,
        grid=(1,),
        in_specs=[out_whole(4 * OWN, D)] * 2 + [ANY] * len(after),
        out_specs=[out_whole(OWN, D)] * 4,
        out_shape=[made((OWN, D), F32)] + [made((OWN, D))] * 3,
        compiler_params=params(12),
        cost_estimate=cost(1 << 20, 6 << 20),
    )(same, got, *far(*after))


def join_halves(same, got, own, ahead, low, high, behind):
    at = 0
    for out in (own, ahead, low, high, behind):
        r = slice(at, at + out.shape[0])
        out[...] = (same[r].astype(F32) + got[r].astype(F32)).astype(out.dtype)
        at += out.shape[0]


def call_join_halves(same, got):
    shapes = [(OWN, F32), (OWN, F32), (OWN // 2, BF), (OWN // 2, BF), (OWN, F32)]
    return pl.pallas_call(
        join_halves,
        grid=(1,),
        in_specs=[out_whole(4 * OWN, D)] * 2,
        out_specs=[out_whole(n, D) for n, _ in shapes],
        out_shape=[made((n, D), t) for n, t in shapes],
        compiler_params=params(12),
        cost_estimate=cost(1 << 20, 6 << 20),
    )(same, got)


def add_halves(ahead, low, behind, high, to_ahead, to_behind):
    half = OWN // 2
    to_ahead[:half, :] = (ahead[:half] + low[...].astype(F32)).astype(BF)
    to_ahead[half:, :] = ahead[half:].astype(BF)
    to_behind[:half, :] = behind[:half].astype(BF)
    to_behind[half:, :] = (behind[half:] + high[...].astype(F32)).astype(BF)


def call_add_halves(ahead, low, behind, high):
    ins = (ahead, low, behind, high)
    return pl.pallas_call(
        add_halves,
        grid=(1,),
        in_specs=[out_whole(*v.shape) for v in ins],
        out_specs=[out_whole(OWN, D)] * 2,
        out_shape=[made((OWN, D))] * 2,
        compiler_params=params(12),
        cost_estimate=cost(1 << 20, 2 << 20),
    )(*ins)


def block_copy(blocks, held, sems, j):
    start = sum(b.shape[0] for b in blocks[:j])
    return pltpu.make_async_copy(
        blocks[j], held.at[pl.ds(start, blocks[j].shape[0])], sems.at[j]
    )


def bring(blocks, held, sems, step=STEP):
    i = pl.program_id(0)

    @pl.when(i == 0)
    def _():
        for j in range(len(blocks)):
            block_copy(blocks, held, sems, j).start()

    for n in range(GROUP // step):

        @pl.when(i == n)
        def _():
            start = 0
            for j, b in enumerate(blocks):
                if start // step == n:
                    block_copy(blocks, held, sems, j).wait()
                start += b.shape[0]

    return held[pl.ds(pl.multiple_of(i * step, step), step), :]


def put_part(at, value, other, same, half=STEPS // 2):
    i = pl.program_id(0)

    @pl.when(i < half)
    def _():
        other[:, at : at + value.shape[1]] = value

    @pl.when(i >= half)
    def _():
        same[:, at : at + value.shape[1]] = value


def rotate(v, cos, sin):
    return v * cos + pltpu.roll(v, HD // 2, 1) * sin


def unrotate(v, cos, sin):
    return v * cos + pltpu.roll(v * sin, HD // 2, 1)


def scores_of(query, key, keep):
    s = last(query, key) * SCALE
    s = jnp.where(keep, s, NEG)
    p = jnp.exp(s - jnp.max(s, axis=-1, keepdims=True))
    return p / jnp.sum(p, axis=-1, keepdims=True)


def keep_mask(doc):
    shape = (SUB, SUB)
    a = lax.broadcasted_iota(jnp.int32, shape, 0)
    b = lax.broadcasted_iota(jnp.int32, shape, 1)
    keep = (doc == doc.T) & (b <= a) & ((b >= SEQ) == (a >= SEQ))
    return jnp.concatenate([keep, keep], axis=0)


def gains_of(w):
    return jnp.sum(w[...].astype(F32), axis=0)


def heads_of(qkv, gains, cos, sin):
    q0, q1, k = qkv[:, :HD], qkv[:, HD:QCOLS], qkv[:, QCOLS : QCOLS + HD]
    gq, gk = gains[0:1], gains[1:2]
    r0, r1, rk = root(q0), root(q1), root(k)
    z0, z1, zk = q0 * r0, q1 * r1, k * rk
    a0 = rotate(z0 * gq, cos, sin).astype(BF)
    a1 = rotate(z1 * gq, cos, sin).astype(BF)
    ak = rotate(zk * gk, cos, sin).astype(BF)
    val = qkv[:, QCOLS + HD :].astype(BF)
    return (r0, r1, rk), (z0, z1, zk), (a0, a1, ak), val


def qkv_matrix(w):
    return w[:, :128, :].reshape(D, CCOLS)


def out_matrix(w, b):
    return w[:, 128 + 16 * b : 144 + 16 * b, :].reshape(QCOLS, WIDE)


ATTN = pl.BlockSpec((16, 192, WIDE), lambda *i: (0, 0, 0), pipeline_mode=pl.Buffered(1))
HEADS = pl.BlockSpec((16, 16, HD), lambda *i: (0, 12, 0), pipeline_mode=pl.Buffered(1))


def attn_forward(*refs):
    blocks, (w_in, heads, cos, sin) = refs[:6], refs[6:10]
    z_out, doc_out, qkv_out, mix_out, other, same, held, sems = refs[-8:]
    rows = bring(blocks, held, sems, 512)
    z, doc = rows[:, :D], rows[:, D:]
    z_out[...] = z
    doc_out[...] = doc
    doc = doc.astype(F32)
    w = w_in[...]
    qkv = plain(z, qkv_matrix(w))
    qkv_out[...] = qkv
    _, _, (a0, a1, ak), val = heads_of(qkv, gains_of(heads), cos[...], sin[...])
    for s in range(512 // SUB):
        r = slice(s * SUB, (s + 1) * SUB)
        p = scores_of(jnp.concatenate([a0[r], a1[r]], axis=0), ak[r], keep_mask(doc[r]))
        o = plain(p.astype(BF), val[r])
        mix_out[r, :HD] = o[:SUB].astype(BF)
        mix_out[r, HD:] = o[SUB:].astype(BF)
    for b in range(4):
        put_part(b * WIDE, plain(mix_out[...], out_matrix(w, b)).astype(BF), other, same, 1)


def norm_back(r, z, gain, e):
    eg = e * gain
    return r * (eg - z * jnp.mean(eg * z, axis=-1, keepdims=True)), jnp.sum(
        e * z, axis=0, keepdims=True
    )


def attn_backward(*refs):
    blocks = refs[:10]
    qkv_in, w_in, heads, doc, cos, sin = refs[10:16]
    g_out, gqkv_out, other, same, gain_out, held, sems = refs[-7:]
    i = pl.program_id(0)
    g = bring(blocks, held, sems)
    g_out[...] = g
    w = w_in[...]
    gm = last(g[:, :WIDE], out_matrix(w, 0))
    for b in range(1, 4):
        gm = gm + last(g[:, b * WIDE : (b + 1) * WIDE], out_matrix(w, b))
    gm = gm.astype(BF)
    gain = gains_of(heads)
    c, s_ = cos[...], sin[...]
    (r0, r1, rk), (z0, z1, zk), (a0, a1, ak), val = heads_of(qkv_in[...], gain, c, s_)
    d0, d1, dk, dv = [], [], [], []
    for s in range(STEP // SUB):
        r = slice(s * SUB, (s + 1) * SUB)
        keep = keep_mask(doc[r, :].astype(F32))
        q = jnp.concatenate([a0[r], a1[r]], axis=0)
        do = jnp.concatenate([gm[r, :HD], gm[r, HD:]], axis=0)
        p = scores_of(q, ak[r], keep)
        dp = last(do, val[r])
        ds = (p * (dp - jnp.sum(p * dp, axis=-1, keepdims=True))).astype(BF)
        dq = plain(ds, ak[r]) * SCALE
        d0.append(dq[:SUB])
        d1.append(dq[SUB:])
        dk.append(first(ds, q) * SCALE)
        dv.append(first(p.astype(BF), do))
    d0, d1, dk, dv = [jnp.concatenate(v, axis=0) for v in (d0, d1, dk, dv)]
    g0, t0 = norm_back(r0, z0, gain[0:1], unrotate(d0, c, s_))
    g1, t1 = norm_back(r1, z1, gain[0:1], unrotate(d1, c, s_))
    gk, tk = norm_back(rk, zk, gain[1:2], unrotate(dk, c, s_))
    gqkv_out[:, :HD] = g0.astype(BF)
    gqkv_out[:, HD:QCOLS] = g1.astype(BF)
    gqkv_out[:, QCOLS : QCOLS + HD] = gk.astype(BF)
    gqkv_out[:, QCOLS + HD :] = dv.astype(BF)
    put_part(0, last(gqkv_out[...], qkv_matrix(w)).astype(BF), other, same)

    @pl.when(i == 0)
    def _():
        gain_out[...] = jnp.zeros_like(gain_out)

    gain_out[0:1] += t0 + t1
    gain_out[1:2] += tk


TABLES = [whole(STEP, HD), whole(STEP, HD)]


def held_rows(width):
    return [pltpu.VMEM((GROUP, width), BF), pltpu.SemaphoreType.DMA((10,))]


def call_forward(blocks, w, cos, sin, after):
    return pl.pallas_call(
        attn_forward,
        grid=(2,),
        in_specs=[ANY] * 6 + [ATTN, HEADS] + [whole(512, HD)] * 2 + [ANY] * len(after),
        out_specs=[
            rows_of(D, 512),
            rows_of(HD, 512),
            rows_of(CCOLS, 512),
            rows_of(QCOLS, 512),
            other_rows(D, 512),
            same_rows(D, 512),
        ],
        scratch_shapes=held_rows(WITH_DOCS),
        out_shape=[
            away((GROUP, D)),
            away((GROUP, HD)),
            away((GROUP, CCOLS), F32),
            away((GROUP, QCOLS)),
            made((GROUP // 2, D)),
            made((GROUP // 2, D)),
        ],
        compiler_params=params(36),
        cost_estimate=cost(2 * GROUP * D * (CCOLS + QCOLS) * 2, 20 << 20),
    )(*far(*blocks, w, w), jnp.tile(cos, (2, 1)), jnp.tile(sin, (2, 1)), *far(*after))


def call_backward(blocks, qkv, w, doc, cos, sin, after):
    return pl.pallas_call(
        attn_backward,
        grid=(STEPS,),
        in_specs=[ANY] * 10
        + [rows_of(CCOLS), ATTN, HEADS, rows_of(HD)]
        + TABLES
        + [ANY] * len(after),
        out_specs=[
            rows_of(D),
            rows_of(CCOLS),
            other_rows(D),
            same_rows(D),
            out_whole(8, HD),
        ],
        scratch_shapes=held_rows(D),
        out_shape=[
            made((GROUP, D)),
            made((GROUP, CCOLS)),
            made((GROUP // 2, D)),
            made((GROUP // 2, D)),
            made((8, HD), F32),
        ],
        compiler_params=params(28),
        cost_estimate=cost(2 * GROUP * D * (CCOLS + QCOLS) * 2, 20 << 20, 5),
    )(*far(*blocks), qkv, *far(w, w), doc, cos, sin, *far(*after))


def ffn_matrix(w, j):
    return w[:, 128 * j : 128 * (j + 1), :].reshape(D, WIDE)


def down_matrix(w, b):
    return w[:, 48 * b : 48 * b + 48, :].reshape(FCOLS, WIDE)


DOWN = pl.BlockSpec((16, 192, WIDE), lambda *i: (0, 2, 0), pipeline_mode=pl.Buffered(1))


def ffn_both(*refs):
    blocks, out_blocks, w_in = refs[:10], refs[10:16], refs[16]
    z_out, g_out, act_out, ggu_out, other, same = refs[17:23]
    held, sems, kept, marks, w, down, w_sems, wide = refs[23:]
    i = pl.program_id(0)

    def w_copy(j):
        if j < 3:
            src = w_in.at[:, pl.ds(128 * j, 128), :]
            dst = w.at[:, :, pl.ds(WIDE * j, WIDE)]
        else:
            src = w_in.at[:, pl.ds(384 + 48 * (j - 3), 48), :]
            dst = down.at[:, :, pl.ds(WIDE * (j - 3), WIDE)]
        return pltpu.make_async_copy(src, dst, w_sems.at[j])

    def arrived(*found):
        @pl.when(i == 0)
        def _():
            for j in found:
                w_copy(j).wait()

    @pl.when(i == 0)
    def _():
        for j in range(7):
            w_copy(j).start()

    z = bring(blocks, held, sems)
    g = bring(out_blocks, kept, marks)
    z_out[...] = z
    g_out[...] = g
    for j in range(3):
        arrived(j)
        cols = slice(j * WIDE, (j + 1) * WIDE)
        wide[:, cols] = plain(z, w[:, :, cols].reshape(D, WIDE))
    arrived(3, 4, 5, 6)
    for n in range(3):
        a, b = slice(n * 256, (n + 1) * 256), slice(FCOLS + n * 256, FCOLS + (n + 1) * 256)
        ga = last(g, down[...].reshape(FCOLS, D)[a])
        gate, up = wide[:, a], wide[:, b]
        sig = jax.nn.sigmoid(gate)
        silu = gate * sig
        act_out[:, a] = (silu * up).astype(BF)
        ggu_out[:, a] = (ga * up * sig * (1.0 + gate * (1.0 - sig))).astype(BF)
        ggu_out[:, b] = (ga * silu).astype(BF)
    for y in range(4):
        part = last(ggu_out[...], w[4 * y : 4 * y + 4].reshape(WIDE, 2 * FCOLS))
        put_part(y * WIDE, part.astype(BF), other, same)


def call_ffn(blocks, out_blocks, w):
    return pl.pallas_call(
        ffn_both,
        grid=(STEPS,),
        in_specs=[ANY] * 17,
        out_specs=[
            rows_of(D),
            rows_of(D),
            rows_of(FCOLS),
            rows_of(2 * FCOLS),
            other_rows(D),
            same_rows(D),
        ],
        scratch_shapes=held_rows(D) * 2
        + [
            pltpu.VMEM((16, 128, 2 * FCOLS), BF),
            pltpu.VMEM((16, 48, D), BF),
            pltpu.SemaphoreType.DMA((7,)),
            pltpu.VMEM((STEP, 2 * FCOLS), F32),
        ],
        out_shape=[
            away((GROUP, D)),
            away((GROUP, D)),
            away((GROUP, FCOLS)),
            away((GROUP, 2 * FCOLS)),
            made((GROUP // 2, D)),
            made((GROUP // 2, D)),
        ],
        compiler_params=params(44),
        cost_estimate=cost(8 * GROUP * D * FCOLS, 30 << 20),
    )(*far(*blocks, *out_blocks, w))


def ffn_grads(z, ggu, act, g, *refs):
    out, down = refs[-2:]
    i = pl.program_id(0)

    for b in range(4):

        @pl.when(i == b)
        def _():
            down[:, b * WIDE : (b + 1) * WIDE] = first(act[...], g[...]).astype(BF)

    @pl.when(i >= 4)
    def _():
        for j in range(3):
            u = first(z[...], ggu[:, j * WIDE : (j + 1) * WIDE]).astype(BF)
            for x in range(4):
                out[x, 128 * j : 128 * (j + 1), :] = u[128 * x : 128 * (x + 1)]
        for x in range(4):
            r = pl.ds(pl.multiple_of(192 * jnp.maximum(i - 4, 0) + 48 * x, 16), 48)
            for b in range(4):
                out[x, 384 + 48 * b : 432 + 48 * b, :] = down[
                    r, b * WIDE : (b + 1) * WIDE
                ]


def call_ffn_grads(z, ggu, act, g, after):
    return pl.pallas_call(
        ffn_grads,
        grid=(8,),
        in_specs=[
            pl.BlockSpec((GROUP, WIDE), lambda i: (0, jnp.maximum(i - 4, 0))),
            whole(GROUP, 2 * FCOLS),
            whole(GROUP, FCOLS),
            pl.BlockSpec((GROUP, WIDE), lambda i: (0, jnp.minimum(i, 3))),
        ]
        + [ANY] * len(after),
        out_specs=pl.BlockSpec(
            (4, FFN_ROWS, WIDE), lambda i: (jnp.maximum(i - 4, 0), 0, 0)
        ),
        scratch_shapes=[pltpu.VMEM((FCOLS, D), BF)],
        out_shape=away((16, FFN_ROWS, WIDE)),
        compiler_params=params(32),
        cost_estimate=cost(6 * GROUP * D * FCOLS, 24 << 20, 20),
    )(*far(z, ggu, act, g, *after))


def ffn_result(act, w_in, *refs):
    other, same = refs[-2:]
    for b in range(4):
        put_part(
            b * WIDE, plain(act[...], down_matrix(w_in, b)).astype(BF), other, same
        )


def call_result(act, w, after):
    return pl.pallas_call(
        ffn_result,
        grid=(STEPS,),
        in_specs=[rows_of(FCOLS), DOWN] + [ANY] * len(after),
        out_specs=[other_rows(D), same_rows(D)],
        out_shape=[made((GROUP // 2, D)), made((GROUP // 2, D))],
        compiler_params=params(24),
        cost_estimate=cost(2 * GROUP * D * FCOLS, 16 << 20),
    )(*far(act, w, *after))


def attn_grads(z, gqkv, mixed, g, gain, *refs):
    out, os = refs[-2:]
    y = pl.program_id(0)

    @pl.when(y == 0)
    def _():
        os[...] = first(mixed[...], g[...]).astype(BF)

    us = first(z[...], gqkv[...]).astype(BF)
    extra = jnp.concatenate([gain[...], jnp.zeros((8, HD), F32)], axis=0).astype(BF)
    for x in range(4):
        r = pl.ds(pl.multiple_of(64 * y + 16 * x, 16), 16)
        out[x, :128, :] = us[128 * x : 128 * (x + 1)]
        for b in range(4):
            out[x, 128 + 16 * b : 144 + 16 * b, :] = os[r, b * WIDE : (b + 1) * WIDE]
        out[x, 192:, :HD] = extra
        out[x, 192:, HD:] = jnp.zeros((16, WIDE - HD), BF)


def call_attn_grads(z, gqkv, mixed, g, gain, after):
    return pl.pallas_call(
        attn_grads,
        grid=(4,),
        in_specs=[
            pl.BlockSpec((GROUP, WIDE), lambda y: (0, y)),
            whole(GROUP, CCOLS),
            whole(GROUP, QCOLS),
            whole(GROUP, D),
            whole(8, HD),
        ]
        + [ANY] * len(after),
        out_specs=pl.BlockSpec((4, ATTN_ROWS, WIDE), lambda y: (y, 0, 0)),
        scratch_shapes=[pltpu.VMEM((QCOLS, D), BF)],
        out_shape=away((16, ATTN_ROWS, WIDE)),
        compiler_params=params(24),
        cost_estimate=cost(2 * GROUP * D * (CCOLS + QCOLS), 16 << 20),
    )(z, gqkv, mixed, g, gain, *far(*after))


def pack_sums(attn, ffn, *refs):
    mine, rows = refs[-2:]
    u = attn[0].astype(F32)
    for k in range(1, 16):
        u = u + attn[k].astype(F32)
    u = u.astype(BF)
    for zh, c in itertools.product(range(2), range(2)):
        r = 32 * (2 * zh + c)
        for zl in range(2):
            at = 4 * zl + 2 * zh + c
            mine[at, :, :WIDE] = u[r : r + 32]
            for j in range(3):
                mine[at, :, WIDE * (j + 1) : WIDE * (j + 2)] = ffn[
                    128 * j + r : 128 * j + r + 32
                ]
            mine[at, :16, 2048:] = u[192:, :HD]
            mine[at, 16:, 2048:] = jnp.zeros((16, HD), BF)
    for b in range(4):
        cols = slice(b * WIDE, (b + 1) * WIDE)
        rows[:16, cols] = u[128 + 16 * b : 144 + 16 * b]
        rows[16:, cols] = ffn[384 + 48 * b : 432 + 48 * b]


def call_pack_sums(attn, ffn, after):
    return pl.pallas_call(
        pack_sums,
        grid=(1,),
        in_specs=[out_whole(16, ATTN_ROWS, WIDE), out_whole(FFN_ROWS, WIDE)]
        + [ANY] * len(after),
        out_specs=[out_whole(8, 32, 2048 + HD), out_whole(64, D)],
        out_shape=[away((8, 32, 2048 + HD)), made((64, D))],
        compiler_params=params(24),
        cost_estimate=cost(1 << 20, 4 << 20),
    )(*far(attn, ffn, *after))


def own_columns(got, w_qkv, w_ffn, gain_in, gain_mid, d_qkv, d_ffn, d_in, d_mid, d_heads):
    for w, gain, out, d_gain, cuts, start in (
        (w_qkv, gain_in, d_qkv, d_in, QKV_CUTS, 0),
        (w_ffn, gain_mid, d_ffn, d_mid, FFN_CUTS, CCOLS),
    ):
        col = column(gain[...].astype(F32))
        total = jnp.zeros((32, 1), F32)
        for begin, width in cuts:
            for zl, c, zh in itertools.product(range(2), range(2), range(2)):
                at = begin + (4 * zl + 2 * c + zh) * width
                u = got[4 * zl + 2 * zh + c, :, start : start + width].astype(F32)
                out[:, at : at + width] = u * col
                total = total + jnp.sum(
                    u * w[:, at : at + width].astype(F32), axis=1, keepdims=True
                )
            start += width
        d_gain[...] = row_of(total)
    heads = got[0, :16, 2048:].astype(F32)
    for r in range(1, 8):
        heads = heads + got[r, :16, 2048:].astype(F32)
    d_heads[...] = heads


def call_own_columns(got, w_qkv, w_ffn, gain_in, gain_mid):
    shapes = [(32, 4096), (32, 2 * FF), (1, 32), (1, 32), (16, HD)]
    ins = (got, w_qkv, w_ffn, gain_in, gain_mid)
    return pl.pallas_call(
        own_columns,
        grid=(1,),
        in_specs=[out_whole(*v.shape) for v in ins],
        out_specs=[out_whole(*v) for v in shapes],
        out_shape=[made(v, F32) for v in shapes],
        compiler_params=params(24),
        cost_estimate=cost(1 << 20, 4 << 20),
    )(*ins)


def own_row_blocks(home, a, b, *refs):
    d_out, d_down = refs[-2:]
    for n in range(2):
        part = jnp.where(home[0] == 1 - n, a[...], b[...]).astype(F32)
        d_out[16 * n : 16 * (n + 1), :] = part[:16]
        d_down[48 * n : 48 * (n + 1), :] = part[16:]


def call_own_row_blocks(home, a, b, after):
    shapes = [(32, D), (96, D)]
    return pl.pallas_call(
        own_row_blocks,
        grid_spec=pltpu.PrefetchScalarGridSpec(
            num_scalar_prefetch=1,
            grid=(1,),
            in_specs=[out_whole(64, D)] * 2 + [ANY] * len(after),
            out_specs=[out_whole(*v) for v in shapes],
        ),
        out_shape=[made(v, F32) for v in shapes],
        compiler_params=params(8),
        cost_estimate=cost(1 << 20, 1 << 20),
    )(home, a, b, *far(*after))


def tables():
    half = HD // 2
    freq = BASE ** (-(np.arange(half, dtype=np.float64) * 2.0 / HD))
    angles = np.arange(SEQ, dtype=np.float64)[:, None] * freq
    cos = np.concatenate([np.cos(angles)] * 2, axis=-1)
    sin = np.concatenate([-np.sin(angles), np.sin(angles)], axis=-1)
    reps = (STEP // SEQ, 1)
    return np.tile(cos, reps).astype(np.float32), np.tile(sin, reps).astype(np.float32)


QKV_CUTS = ((0, QCOLS), (H * HD, HD), ((H + KVH) * HD, HD))
FFN_CUTS = ((0, FCOLS), (FF, FCOLS))
EXTRA = CCOLS + HD


def split_weights(at, w_qkv, w_ffn, gain_in, gain_mid, g_query, g_key, *outs):
    spot = lax.broadcasted_iota(jnp.int32, (1, HD), 1) - 2 * at[4]
    heads = [
        jnp.where(spot == 0, g[:, :1], jnp.where(spot == 1, g[:, 1:], 0.0))
        for g in (g_query[...].astype(F32), g_key[...].astype(F32))
    ]
    heads = jnp.concatenate(heads + [jnp.zeros((30, HD), F32)], axis=0).astype(BF)
    col_in = column(gain_in[...].astype(F32))
    col_mid = column(gain_mid[...].astype(F32))
    for n in range(4):
        attn, ffn = outs[n // 2].at[n % 2], outs[2 + n // 2].at[n % 2]
        for w, col, out, cuts in (
            (w_qkv, col_in, attn, QKV_CUTS),
            (w_ffn, col_mid, ffn, FFN_CUTS),
        ):
            start = 0
            for begin, width in cuts:
                from_ = pl.multiple_of(begin + at[n] * width, 128)
                part = w[:, pl.ds(from_, width)].astype(F32) * col
                out[:, start : start + width] = part.astype(BF)
                start += width
        attn[:, CCOLS:] = heads


def call_split_weights(at, w_qkv, w_ffn, gain_in, gain_mid, g_query, g_key):
    ins = (w_qkv, w_ffn, gain_in, gain_mid, g_query, g_key)
    shapes = [(2, 32, EXTRA)] * 2 + [(2, 32, 2 * FCOLS)] * 2
    return pl.pallas_call(
        split_weights,
        grid_spec=pltpu.PrefetchScalarGridSpec(
            num_scalar_prefetch=1,
            grid=(1,),
            in_specs=[out_whole(*v.shape) for v in ins],
            out_specs=[out_whole(*v) for v in shapes],
        ),
        out_shape=[made(v) for v in shapes],
        compiler_params=params(12),
        cost_estimate=cost(1 << 20, 2 << 20),
    )(at, *far(*ins))


def pack_first(at, near, got, far, rows, out):
    blocks = (near[0], got[0], far[0], far[1])
    for n, block in enumerate(blocks):
        zh, c = at[0] ^ (n // 2), at[1] ^ (n % 2)
        begin = pl.multiple_of(64 * zh + 32 * c, 32)
        out[pl.ds(begin, 32), :] = block[:, :CCOLS]
    for b in range(4):
        out[128 + 16 * b : 144 + 16 * b, :] = rows[:, b * WIDE : (b + 1) * WIDE]
    heads = sum(block[:16, CCOLS:].astype(F32) for block in blocks)
    out[192:, :HD] = heads.astype(BF)
    out[192:, HD:] = jnp.zeros((16, WIDE - HD), BF)


def pack_second(at, near, got, far, rows, *refs):
    out = refs[-1]
    for n, block in enumerate((near[0], got[0], far[0], far[1])):
        zh, c = at[0] ^ (n // 2), at[1] ^ (n % 2)
        for j in range(3):
            begin = pl.multiple_of(128 * j + 64 * zh + 32 * c, 32)
            out[pl.ds(begin, 32), :] = block[:, j * WIDE : (j + 1) * WIDE]
    for b in range(4):
        out[384 + 48 * b : 432 + 48 * b, :] = rows[:, b * WIDE : (b + 1) * WIDE]


def call_pack(body, at, total, *ins, after=()):
    return pl.pallas_call(
        body,
        grid_spec=pltpu.PrefetchScalarGridSpec(
            num_scalar_prefetch=1,
            grid=(1,),
            in_specs=[out_whole(*v.shape) for v in ins] + [ANY] * len(after),
            out_specs=out_whole(total, WIDE),
        ),
        out_shape=made((total, WIDE)),
        compiler_params=params(12),
        cost_estimate=cost(1 << 20, 2 << 20),
    )(at, *ins, *far(*after))


def fold(v):
    return jnp.concatenate(
        [v[:, i : i + WIDE] for i in range(0, v.shape[1], WIDE)], axis=0
    )


def layer(
    tokens,
    segments,
    qkv_weight,
    out_weight,
    attn_gain,
    query_gain,
    key_gain,
    ffn_weight,
    down_weight,
    ffn_gain,
    out_grad,
):
    zl, y, zh, x, c = [lax.axis_index(a) for a in AXES]
    seqs = tokens.shape[0]
    x_own = tokens.reshape(OWN, D)
    g_own = out_grad.reshape(OWN, D)
    cos, sin = tables()

    f = ((y * 2 + zh) * 4 + x) * 2 + c
    gain_in, gain_mid = attn_gain.reshape(1, 32), ffn_gain.reshape(1, 32)
    near, distant = 4 * zl + zh, 4 * (1 - zl) + (1 - zh)
    at = jnp.stack(
        [near + 2 * c, distant + 2 * c, near + 2 * (1 - c), distant + 2 * (1 - c), f]
    ).astype(jnp.int32)
    attn_keep, attn_give, ffn_keep, ffn_give = call_split_weights(
        at,
        qkv_weight,
        ffn_weight,
        gain_in,
        gain_mid,
        query_gain.reshape(1, 2),
        key_gain.reshape(1, 2),
    )
    attn_got = send(attn_give, step("c", 1))
    attn_far = send(jnp.stack([attn_keep[1], attn_got[1]]), partner)
    home = (y // 2) == zl
    here = jnp.stack([zh, c]).astype(jnp.int32)
    pack = call_pack(
        pack_first,
        here,
        ATTN_ROWS,
        attn_keep,
        attn_got,
        attn_far,
        give_rows(out_weight, home),
    )
    w_first = lax.all_gather(pack, ("y", "x"), axis=0, tiled=False)
    z_own = call_own_norm(x_own, segments.reshape(1, OWN))
    z_same, out_same = relay(z_own), relay(g_own)
    in_blocks = all_at_once(z_same)
    ffn_got = send(ffn_give, step("c", 1))
    ffn_far = send(jnp.stack([ffn_keep[1], ffn_got[1]]), partner)
    pack = call_pack(
        pack_second,
        here,
        FFN_ROWS,
        ffn_keep,
        ffn_got,
        ffn_far,
        give_rows(down_weight, home),
        after=z_same[1:] + out_same[1:],
    )
    w_second = lax.all_gather(pack, ("y", "x"), axis=0, tiled=False)

    out_blocks = all_at_once(out_same)
    z_in, doc, qkv, mixed, other, same = call_forward(
        in_blocks, w_first, cos, sin, out_same[1:]
    )
    parts, _ = sum_relay(other, same)
    hidden, z_own = call_own(
        own_middle, [x_own] + parts, [F32, BF]
    )
    z_blocks = gather_group(z_own)
    z_mid, g_all, active, g_gate_up, other, same = call_ffn(
        z_blocks, out_blocks, w_second
    )

    parts, sent = sum_group(other, same)
    ffn_sum = call_ffn_grads(z_mid, g_gate_up, active, g_all, (sent,))
    g_hidden, g_low = call_own(
        functools.partial(own_back, 2, 4),
        [hidden, g_own] + parts,
        [F32, BF],
        (ffn_sum,),
        250000,
    )
    g_blocks = gather_group(g_low)
    g_low, g_qkv, other, same, gain_part = call_backward(
        g_blocks, qkv, w_first, doc, cos, sin, ()
    )
    parts, sent = sum_relay(other, same)
    (g_tokens,) = call_own(
        functools.partial(own_back, 1, 3), [x_own, g_hidden] + parts, [F32]
    )
    result_other, result_same = call_result(active, w_second, (sent,))
    result_parts, _ = sum_relay(result_other, result_same)
    (result,) = call_own(own_result, [hidden] + result_parts, [BF])

    ffn_sum = lax.psum_scatter(
        ffn_sum.reshape(16 * FFN_ROWS, WIDE), ("y", "x"), scatter_dimension=0, tiled=True
    )
    attn_sum = call_attn_grads(z_in, g_qkv, mixed, g_low, gain_part, (sent,))
    attn_sum = lax.all_to_all(attn_sum, ("y", "x"), 0, 0, tiled=True)
    mine, rows = call_pack_sums(attn_sum, ffn_sum, (g_tokens, result))
    got = lax.all_to_all(mine, ("zl", "zh", "c"), 0, 0, tiled=True)
    d_qkv, d_ffn, d_in, d_mid, gain_sum = call_own_columns(
        got, qkv_weight, ffn_weight, gain_in, gain_mid
    )
    gain_own = lax.dynamic_slice(gain_sum, (0, 2 * f), (2, 2))
    d_out, d_down = call_own_row_blocks(
        home.astype(jnp.int32).reshape(1), *take_rows(rows), (d_in,)
    )

    return (
        result.reshape(seqs, SEQ, D),
        g_tokens.reshape(seqs, SEQ, D),
        d_qkv,
        d_out,
        d_in[0],
        gain_own[0],
        gain_own[1],
        d_ffn,
        d_down,
        d_mid[0],
    )


def give_rows(shard, home):
    half = shard.shape[0] // 2
    return send(jnp.where(home, shard[:half], shard[half:]), spread_rows)


def take_rows(v):
    mine = send(v, collect_rows)
    return mine, send(mine, other_plane)


def solution(mesh):
    fine = Mesh(mesh.devices.reshape([SIZES[a] for a in AXES]), AXES)
    batch = AXES
    shard = ("y", "zh", "x", "c")
    matrix = P(shard, None)
    vector = P(shard)
    return jax.shard_map(
        layer,
        mesh=fine,
        in_specs=(
            P(batch, None, None),
            P(batch, None),
            matrix,
            matrix,
            vector,
            vector,
            vector,
            matrix,
            matrix,
            vector,
            P(batch, None, None),
        ),
        out_specs=(
            P(batch, None, None),
            P(batch, None, None),
            matrix,
            matrix,
            vector,
            vector,
            vector,
            matrix,
            matrix,
            vector,
        ),
        check_vma=False,
    )
```
